256 devices in a mesh: row: 8 (over x_lo, y), col: 16 (over z, x_hi), srv: 2 (over core).
Axes of the slice: x: 4 (x_hi: 2, x_lo: 2; x = x_hi * 2 + x_lo), y: 4, z: 8, core: 2. Of those that a mesh axis runs over, the one named last changes fastest.
Arguments:
- inputs: bfloat16 [8192, 8192], P(('row', 'srv'), 'col'), may hold values from -0.75 to 0.75
- grad_out: bfloat16 [8192, 8192], P(('row', 'srv'), 'col'), may hold values from -6 to 6
- weight: bfloat16 [8192, 8192], P('col', 'row'), may hold values from -0.0625 to 0.0625
- blocks: int32 [16, 128, 2], P('col'), may hold values from -1 to 63, as said below
- owner: int32 [16, 128], P('col'), may hold values from -1 to 15, as said below
Outputs:
- grad_in: bfloat16 [8192, 8192], P(('row', 'srv'), 'col')
- pushed: float32 [16, 128, 128, 128], P(('row', 'srv'), 'col')
The draws below stay inside these ranges and needn't reach their ends.
Inputs may be any that keep to these rules, and one draw needn't show every extreme that they name: List g holds distinct blocks whose row block lies in g * 8192 / 2048 to (g + 1) * 8192 / 2048 - 1; live entries come first, the rest are (-1, -1); some list is full, and each list has 8 or more live entries. An entry that is not live has owner -1; no owner gets more than 8 live entries of one list, and in a full list every owner gets exactly 8.
All inputs are finite; a program needn't handle non-finite values.
Results may differ from the reference program's by a relative error of at most 0.001.
Values may be sent and summed in bfloat16 or wider, within the bound.
No kernel may reach another device: no remote copies, remote signals or barrier semaphores. Data moves between devices by JAX's collectives and lax.ppermute only.
A program may use at most 128 MiB of HBM per device.

```python
import jax
import jax.numpy as jnp
from jax import lax

DIN = 8192
DOUT = 8192
BLK = 128
CAP = 8
GROUPS = 16
OWNERS = 16
MAXB = 128
EXAMPLES = 8192


def shared_lists(key):
    row_blocks = DIN // (GROUPS * BLK)
    col_blocks = DOUT // BLK
    base = jax.random.randint(jax.random.fold_in(key, 11), (GROUPS,), CAP, MAXB + 1)
    fullest = jax.random.randint(jax.random.fold_in(key, 12), (), 0, GROUPS)
    counts = jnp.where(jnp.arange(GROUPS) == fullest, MAXB, base)
    picks = jax.vmap(lambda k: jax.random.permutation(k, row_blocks * col_blocks))(jax.random.split(jax.random.fold_in(key, 13), GROUPS))[:, :MAXB]
    seats = jax.vmap(lambda k: jax.random.permutation(k, MAXB))(jax.random.split(jax.random.fold_in(key, 14), GROUPS))
    live = jnp.arange(MAXB)[None, :] < counts[:, None]
    row_ids = jnp.arange(GROUPS)[:, None] * row_blocks + picks // col_blocks
    col_ids = picks % col_blocks
    listed = jnp.stack([jnp.where(live, row_ids, -1), jnp.where(live, col_ids, -1)], axis=2)
    owners = jnp.where(live, seats // CAP, -1)
    return (listed.astype(jnp.int32), owners.astype(jnp.int32))


def draw_blocks(key, part):
    listed, owners = shared_lists(key)
    return listed


def draw_owner(key, part):
    listed, owners = shared_lists(key)
    return owners


def block_levels(rng, extent, cuts, least, top_value):
    def one(dim, parts):
        draws = jax.random.uniform(jax.random.fold_in(jax.random.fold_in(rng, 6), dim), (parts,), jnp.float32, least / len(cuts), top_value / len(cuts))
        return jnp.repeat(jnp.exp(draws), extent[dim] // parts).reshape((-1,) + (1,) * (len(extent) - dim - 1))

    loudness = one(*cuts[0])
    for cut in cuts[1:]:
        loudness = loudness * one(*cut)
    return loudness


def noise(key, dims, spread, most, pieces=(), kind=jnp.bfloat16):
    values = jax.random.normal(key, dims, jnp.float32) * spread
    if len(pieces) > 0:
        values = block_levels(key, dims, pieces, -0.22, 0.18) * values
    return jnp.clip(values, min=-most, max=most).astype(kind)


def setup_inputs(seed: int = 0) -> dict:
    key_of = jax.random.split(jax.random.key(seed), 6)
    inputs = noise(key_of[0], (EXAMPLES, DIN), 0.125, 0.75, ((0, 16), (1, 16)))
    grad_out = noise(key_of[1], (EXAMPLES, DOUT), 1.0, 6.0, ((0, 16), (1, 16)))
    weight = noise(key_of[2], (DIN, DOUT), DIN ** -0.5, 0.0625, ((0, 16), (1, 8)))
    blocks = draw_blocks(jax.random.fold_in(key_of[5], 71), 0)
    owner = draw_owner(jax.random.fold_in(key_of[5], 71), 0)
    return dict(inputs=inputs, grad_out=grad_out, weight=weight, blocks=blocks, owner=owner)


def reference(inputs, grad_out, weight, blocks, owner):
    grad_in = jnp.dot(grad_out, weight.T, preferred_element_type=jnp.float32).astype(jnp.bfloat16)
    live = blocks[:, :, 0] >= 0
    same = owner[:, :, None] == owner[:, None, :]
    order = jnp.arange(MAXB, dtype=jnp.int32)
    earlier = order[None, :] < order[:, None]
    rank = jnp.sum((same & earlier[None] & live[:, None, :]).astype(jnp.int32), axis=2)
    row_ids = jnp.maximum(blocks[:, :, 0], 0).astype(jnp.int32)
    col_ids = jnp.maximum(blocks[:, :, 1], 0).astype(jnp.int32)

    def one_tile(entry):
        row_id, col_id, weight_live = entry
        left = lax.dynamic_slice_in_dim(inputs, (row_id * BLK).astype(jnp.int32), BLK, 1)
        right = lax.dynamic_slice_in_dim(grad_out, (col_id * BLK).astype(jnp.int32), BLK, 1)
        return jnp.dot(left.T, right, preferred_element_type=jnp.float32) * weight_live

    tiles = lax.map(one_tile, (row_ids.reshape(-1), col_ids.reshape(-1), live.reshape(-1).astype(jnp.float32)))
    slots = (jnp.arange(GROUPS, dtype=jnp.int32)[:, None] * CAP + rank).astype(jnp.int32)
    owners = jnp.maximum(owner, 0).astype(jnp.int32)
    pushed = jnp.zeros((OWNERS, GROUPS * CAP, BLK, BLK), jnp.float32)
    pushed = pushed.at[owners.reshape(-1), slots.reshape(-1)].add(tiles)
    return grad_in, pushed
```

```python
import functools

import jax
import jax.numpy as jnp
from jax import lax
from jax.experimental import pallas as pl
from jax.experimental.pallas import tpu as pltpu
from jax.sharding import PartitionSpec as P

BLK = 128
CAP = 8
POWER = 9
TOP = 13.0
TAIL = 16
F32 = jnp.float32
BF16 = jnp.bfloat16

COLS = ((0, 0), (-1, 0), (1, 0), (0, 1), (-2, 0), (2, 0), (-3, 0), (3, 0),
        (4, 0), (-1, 1), (1, 1), (-2, 1), (2, 1), (-3, 1), (3, 1), (4, 1))
ROWS = ((0, 0), (1, 0), (0, -1), (1, -1), (0, 1), (1, 1), (0, 2), (1, 2))
DESTS = ((1, 0), (1, 1), (1, 3), (1, 2), (0, 1), (0, 3), (0, 2), (0, 0))


def z_shift(d):
    return [(z * 2 + h, ((z + d) % 8) * 2 + h) for z in range(8) for h in range(2)]


def row_shift(dx, dy):
    return [(l * 4 + y, (l ^ dx) * 4 + (y + dy) % 4) for l in range(2) for y in range(4)]


X_SWAP = [(z * 2 + h, z * 2 + 1 - h) for z in range(8) for h in range(2)]
CORE_SWAP = [(0, 1), (1, 0)]


def any_spec():
    return pl.BlockSpec(memory_space=pl.ANY)


def smem_spec():
    return pl.BlockSpec(memory_space=pltpu.SMEM)


def vmem_spec():
    return pl.BlockSpec(memory_space=pltpu.VMEM)


def params(mib):
    return pltpu.CompilerParams(vmem_limit_bytes=mib * 1024 * 1024)


def dense_kernel(count, first, where_ref, xt_ref, *refs):
    blocks = refs[:count]
    out, made, sems = refs[count + (0 if first else 1):]
    copies = []
    for j in range(count):
        acc = jnp.dot(xt_ref[...], blocks[j][...], preferred_element_type=F32)
        for cc in range(4):
            for rb in range(4):
                made[j, cc * 4 + rb] = acc[rb * BLK:(rb + 1) * BLK, cc * BLK:(cc + 1) * BLK]
        copy = pltpu.make_async_copy(made.at[j], out.at[where_ref[j]], sems.at[j])
        copy.start()
        copies.append(copy)
    for copy in copies:
        copy.wait()


def dense(total, where, xt, blocks):
    count = len(blocks)
    first = total is None
    args = [where, xt, *blocks] + ([] if first else [total])
    return pl.pallas_call(
        functools.partial(dense_kernel, count, first),
        out_shape=jax.ShapeDtypeStruct((16, 16, BLK, BLK), F32),
        in_specs=[smem_spec()] + [vmem_spec()] * (1 + count) + ([] if first else [any_spec()]),
        out_specs=any_spec(),
        scratch_shapes=[pltpu.VMEM((count, 16, BLK, BLK), F32), pltpu.SemaphoreType.DMA((count,))],
        input_output_aliases={} if first else {2 + count: 0},
        compiler_params=params(24),
        cost_estimate=pl.CostEstimate(
            flops=count * 2 * 512 ** 3, bytes_accessed=count * 3 * 512 * 1024, transcendentals=0),
    )(*args)


def pick_kernel(chunks, slot_ref, row_ref, total, out, sems):
    def place(i):
        return jnp.maximum(slot_ref[row_ref[i // CAP] * CAP + i % CAP], 0)

    def start(i, carry):
        pltpu.make_async_copy(total.at[place(i)], out.at[i], sems.at[i]).start()
        return carry

    def finish(i, carry):
        pltpu.make_async_copy(total.at[place(i)], out.at[i], sems.at[i]).wait()
        return carry

    lax.fori_loop(0, chunks * CAP, start, 0)
    lax.fori_loop(0, chunks * CAP, finish, 0)


def pick(slots, owners, total):
    chunks = owners.shape[0]
    return pl.pallas_call(
        functools.partial(pick_kernel, chunks),
        out_shape=jax.ShapeDtypeStruct((chunks * CAP, BLK, BLK), F32),
        in_specs=[smem_spec(), smem_spec(), any_spec()],
        out_specs=any_spec(),
        scratch_shapes=[pltpu.SemaphoreType.DMA((chunks * CAP,))],
        compiler_params=params(16),
        cost_estimate=pl.CostEstimate(
            flops=0, bytes_accessed=chunks * CAP * BLK * BLK * 8, transcendentals=0),
    )(slots, owners, total)


def code_kernel(coded, plain, slot_ref, row_ref, total, other, *refs):
    chunks = coded + plain
    outs = refs[:chunks]
    mine, theirs, my_sems, their_sems = refs[chunks:]

    def place(i):
        return jnp.maximum(slot_ref[row_ref[i // CAP] * CAP + i % CAP], 0)

    def mine_copy(i):
        return pltpu.make_async_copy(total.at[place(i)], mine.at[i], my_sems.at[i])

    def theirs_copy(m):
        part = pl.ds(m * CAP, CAP)
        return pltpu.make_async_copy(other.at[part], theirs.at[part], their_sems.at[m])

    def start(i, carry):
        mine_copy(i).start()
        return carry

    def finish(i, carry):
        mine_copy(i).wait()
        return carry

    for m in range(chunks):
        theirs_copy(m).start()
        lax.fori_loop(m * CAP, (m + 1) * CAP, start, 0)
    for m in range(chunks):
        theirs_copy(m).wait()
        lax.fori_loop(m * CAP, (m + 1) * CAP, finish, 0)
        most = jnp.zeros((1, BLK), F32)
        for t in range(CAP):
            i = m * CAP + t
            live = slot_ref[row_ref[m] * CAP + t] >= 0
            both = jnp.where(live, mine[i] + theirs[i], 0.0)
            if m >= coded:
                outs[m][t] = both
            else:
                mine[i] = both
                most = jnp.maximum(most, jnp.max(jnp.abs(both), axis=0, keepdims=True))
        if m < coded:
            level = jnp.ceil(jnp.log2(jnp.maximum(most, 1e-30)))
            scale = jnp.exp2(TOP - level)
            for t in range(CAP):
                v = mine[m * CAP + t] * scale
                v2 = v * v
                v4 = v2 * v2
                outs[m][t * BLK:(t + 1) * BLK, :] = (v4 * v4 * v).astype(BF16)
            outs[m][CAP * BLK:, :] = jnp.broadcast_to(level, (TAIL, BLK)).astype(BF16)


def code(slots, owners, total, other, coded):
    chunks = owners.shape[0]
    plain = chunks - coded
    return pl.pallas_call(
        functools.partial(code_kernel, coded, plain),
        out_shape=[jax.ShapeDtypeStruct((CAP * BLK + TAIL, BLK), BF16)] * coded
        + [jax.ShapeDtypeStruct((CAP, BLK, BLK), F32)] * plain,
        in_specs=[smem_spec(), smem_spec(), any_spec(), any_spec()],
        out_specs=[vmem_spec()] * chunks,
        scratch_shapes=[
            pltpu.VMEM((chunks * CAP, BLK, BLK), F32),
            pltpu.VMEM((chunks * CAP, BLK, BLK), F32),
            pltpu.SemaphoreType.DMA((chunks * CAP,)),
            pltpu.SemaphoreType.DMA((chunks,)),
        ],
        compiler_params=params(24),
        cost_estimate=pl.CostEstimate(
            flops=chunks * CAP * BLK * BLK * 8, bytes_accessed=chunks * CAP * BLK * BLK * 10,
            transcendentals=0),
    )(slots, owners, total, other)


def sum_kernel(own, *refs):
    arrived, out = refs[:-1], refs[-1]
    scales = []
    for ref in arrived:
        level = ref[CAP * BLK:CAP * BLK + TAIL, :].astype(F32)[0:1, :]
        scales.append(level - TOP)
    for t in range(CAP):
        acc = own[t]
        for ref, scale in zip(arrived, scales):
            y = ref[t * BLK:(t + 1) * BLK, :].astype(F32)
            size = jnp.exp2(jnp.log2(jnp.maximum(jnp.abs(y), 1e-37)) * (1.0 / POWER) + scale)
            size = jnp.where(jnp.abs(y) > 1e-37, size, 0.0)
            acc = acc + jnp.where(y < 0, -size, size)
        out[t] = acc


def total_sum(own, arrived):
    return pl.pallas_call(
        sum_kernel,
        out_shape=jax.ShapeDtypeStruct((CAP, BLK, BLK), F32),
        in_specs=[vmem_spec()] * (1 + len(arrived)),
        out_specs=vmem_spec(),
        compiler_params=params(24),
        cost_estimate=pl.CostEstimate(
            flops=8 * CAP * BLK * BLK * 8, bytes_accessed=8 * CAP * BLK * BLK * 2,
            transcendentals=0),
    )(own, *arrived)


def grad_kernel(row_of_ref, half_ref, mine, theirs, *refs):
    blocks = refs[:16]
    out, grads, weights, g_sems, w_sems = refs[16:]
    side = half_ref[0]
    core = half_ref[1]
    w_copies = [
        pltpu.make_async_copy(mine, weights.at[core], w_sems.at[0]),
        pltpu.make_async_copy(theirs, weights.at[1 - core], w_sems.at[1]),
    ]
    g_copies = [pltpu.make_async_copy(blocks[k], grads.at[k], g_sems.at[k]) for k in range(16)]
    for copy in w_copies + g_copies:
        copy.start()
    for copy in w_copies:
        copy.wait()
    acc = jnp.zeros((512, 512), F32)
    for k, (dz, dxh) in enumerate(COLS):
        g_copies[k].wait()
        row = row_of_ref[dz % 8]
        first = pl.multiple_of((side if dxh == 0 else 1 - side) * 512, 512)
        w = weights[:, row, :, pl.ds(first, 512)].reshape(512, 512)
        acc = acc + lax.dot_general(
            grads[k], w, (((1,), (1,)), ((), ())), preferred_element_type=F32)
    out[...] = acc.astype(BF16)


def grad_in_of(row_of, half, mine, theirs, blocks):
    return pl.pallas_call(
        grad_kernel,
        out_shape=jax.ShapeDtypeStruct((512, 512), BF16),
        in_specs=[smem_spec(), smem_spec()] + [any_spec()] * 18,
        out_specs=vmem_spec(),
        scratch_shapes=[
            pltpu.VMEM((16, 512, 512), BF16),
            pltpu.VMEM((2, 8, 256, 1024), BF16),
            pltpu.SemaphoreType.DMA((16,)),
            pltpu.SemaphoreType.DMA((2,)),
        ],
        compiler_params=params(40),
        cost_estimate=pl.CostEstimate(
            flops=2 * 512 * 512 * 8192, bytes_accessed=17 * 1024 * 1024, transcendentals=0),
    )(row_of, half, mine, theirs, *blocks)


def body(inputs, grad_out, weight, blocks, owner):
    row = lax.axis_index("row")
    col = lax.axis_index("col")
    core = lax.axis_index("srv")
    x_lo, y = row // 4, row % 4
    z, x_hi = col // 2, col % 2

    def up(v):
        return lax.ppermute(v, "col", z_shift(1))

    def down(v):
        return lax.ppermute(v, "col", z_shift(-1))

    def across(v):
        return lax.ppermute(v, "col", X_SWAP)

    def to_row(v, dx, dy):
        return lax.ppermute(v, "row", row_shift(dx, dy))

    def to_core(v):
        return lax.ppermute(v, "srv", CORE_SWAP)

    o0 = across(grad_out)
    a1, c1 = up(grad_out), down(grad_out)
    a2, c2 = up(a1), down(c1)
    oa2, oc2 = across(a2), across(c2)
    a3, c3 = up(a2), down(c2)
    f4 = jnp.concatenate([up(a3[:256]), down(c3[256:])], axis=0)
    o4 = across(f4)
    e1, f1 = up(o0), down(o0)
    e3, f3 = up(oa2), down(oc2)
    cols = [grad_out, a1, c1, o0, a2, c2, a3, c3, f4, e1, f1, oa2, oc2, e3, f3, o4]

    half = lax.dynamic_slice_in_dim(weight, core * 256, 256, 0)
    pair = jnp.concatenate([half, to_row(half, 1, 0)], axis=0)
    wa, wc = to_row(pair, 0, 1), to_row(pair, 0, -1)
    wd, we = to_row(wa[:256], 0, 1), to_row(wc[256:], 0, -1)
    w_mine = jnp.concatenate([pair, wa, wc, wd, we], axis=0).reshape(8, 256, 1024)
    w_theirs = to_core(w_mine)

    listed = blocks[0]
    owners = owner[0]
    live = listed[:, 0] >= 0
    order = jnp.arange(listed.shape[0], dtype=jnp.int32)
    same = owners[:, None] == owners[None, :]
    earlier = order[None, :] < order[:, None]
    rank = jnp.sum((same & earlier & live[None, :]).astype(jnp.int32), axis=1)
    position = jnp.where(live, owners * CAP + rank, -1)
    tile = jnp.where(live, listed[:, 1] * 4 + listed[:, 0] % 4, 0)
    fills = position[None, :] == order[:, None]
    slots = jnp.sum(jnp.where(fills, tile[None, :] + 1, 0), axis=1) - 1

    def col_index(first, last):
        return jnp.stack([((z + dz) % 8) * 2 + (x_hi ^ dxh) for dz, dxh in COLS[first:last]]).astype(jnp.int32)

    xt = inputs.T
    total = None
    for first, last in ((0, 1), (1, 4), (4, 6), (6, 8), (8, 13), (13, 16)):
        total = dense(total, col_index(first, last), xt, cols[first:last])
    total = total.reshape(256, BLK, BLK)

    dest_rows = [(x_lo ^ dx) * 4 + (y + dy) % 4 for dx, dy in DESTS]
    mine_owners = jnp.stack([r * 2 + core for r in dest_rows]).astype(jnp.int32)
    their_owners = jnp.stack([r * 2 + 1 - core for r in dest_rows]).astype(jnp.int32)
    other_far = to_core(pick(slots, their_owners[:4], total))
    other_near = to_core(pick(slots, their_owners[4:], total))
    far = code(slots, mine_owners[:4], total, other_far, 4)
    near = code(slots, mine_owners[4:], total, other_near, 3)
    coded = list(far) + list(near[:3])
    arrived = [to_row(v, dx, dy) for v, (dx, dy) in zip(coded, DESTS)]
    pushed = total_sum(near[3], arrived)

    row_ids = jnp.stack([(x_lo ^ dx) * 4 + (y + dy) % 4 for dx, dy in ROWS])
    wanted = (z + jnp.arange(8)) % 8
    row_of = jnp.argmax(row_ids[None, :] == wanted[:, None], axis=1).astype(jnp.int32)
    sides = jnp.stack([x_hi, core]).astype(jnp.int32)
    grad_in = grad_in_of(row_of, sides, w_mine, w_theirs, cols)
    return grad_in, pushed.reshape(1, CAP, BLK, BLK)


def solution(mesh):
    in_specs = (
        P(("row", "srv"), "col"),
        P(("row", "srv"), "col"),
        P("col", "row"),
        P("col", None, None),
        P("col", None),
    )
    out_specs = (P(("row", "srv"), "col"), P(("row", "srv"), "col", None, None))
    return jax.shard_map(body, mesh=mesh, in_specs=in_specs, out_specs=out_specs, check_vma=False)
```

```python
import functools

import jax
import jax.numpy as jnp
import numpy as np
from jax import lax
from jax.experimental import pallas as pl
from jax.experimental.pallas import tpu as pltpu
from jax.sharding import PartitionSpec as P

BLK = 128
CAP = 8
POWER = 9
TOP = 13.0
TAIL = 16
F32 = jnp.float32
BF16 = jnp.bfloat16

COLS = ((0, 0), (-1, 0), (1, 0), (-2, 0), (2, 0), (0, 1), (-3, 0), (3, 0), (-2, 1),
        (-4, 0), (-1, 1), (1, 1), (2, 1), (-3, 1), (3, 1), (-4, 1))
LAST = 13
DESTS = ((1, 0), (1, 1), (1, 3), (1, 2), (0, 2), (0, 1), (0, 3), (0, 0))
EARLY = 2
DENSE_MIB = PICK_MIB = CODE_MIB = GRAD_MIB = 20
COL_AT, ROW_AT, SIDE_AT, MINE_AT, THEIRS_AT, SLOT_AT = 0, 16, 48, 50, 58, 66


def z_shift(d):
    return [((z * 2 + h) * 2 + c, (((z + (1 - 2 * c) * d) % 8) * 2 + h) * 2 + c)
            for z in range(8) for h in range(2) for c in range(2)]


def y_shift(d):
    return [((l * 4 + y) * 2 + c, (l * 4 + (y + (1 - 2 * c) * d) % 4) * 2 + c)
            for l in range(2) for y in range(4) for c in range(2)]


def row_shift(dx, dy):
    return [(l * 4 + y, (l ^ dx) * 4 + (y + dy) % 4) for l in range(2) for y in range(4)]


X_SWAP = [(z * 2 + h, z * 2 + 1 - h) for z in range(8) for h in range(2)]
CORE_SWAP = [(0, 1), (1, 0)]


def hbm_spec():
    return pl.BlockSpec(memory_space=pltpu.HBM)


def smem_spec():
    return pl.BlockSpec(memory_space=pltpu.SMEM)


def vmem_spec():
    return pl.BlockSpec(memory_space=pltpu.VMEM)


def params(mib):
    return pltpu.CompilerParams(vmem_limit_bytes=mib * 1024 * 1024)


def dense_kernel(count, place, first, table, xt_ref, *refs):
    blocks = refs[:count]
    out = refs[count + (0 if first else 1)]
    for j in range(count):
        acc = jnp.dot(xt_ref[...], blocks[j][...], preferred_element_type=F32)
        at = table[COL_AT + place + j] * 16
        for cc in range(4):
            for rb in range(4):
                out[at + cc * 4 + rb] = acc[rb * BLK:(rb + 1) * BLK, cc * BLK:(cc + 1) * BLK]


def dense(total, table, xt, blocks, place):
    count = len(blocks)
    first = total is None
    args = [table, xt, *blocks] + ([] if first else [total])
    return pl.pallas_call(
        functools.partial(dense_kernel, count, place, first),
        out_shape=jax.ShapeDtypeStruct((256, BLK, BLK), F32),
        in_specs=[smem_spec(), vmem_spec()] + [vmem_spec()] * count + ([] if first else [vmem_spec()]),
        out_specs=vmem_spec(),
        input_output_aliases={} if first else {2 + count: 0},
        compiler_params=params(DENSE_MIB),
        cost_estimate=pl.CostEstimate(
            flops=count * 2 * 512 ** 3, bytes_accessed=count * 3 * 512 * 1024, transcendentals=0),
    )(*args)


def slot_tile(table, owner_at, i):
    return table[SLOT_AT + table[owner_at + i // CAP] * CAP + i % CAP]


def pick_kernel(first, chunks, table, total, out):
    for i in range(chunks * CAP):
        out[i] = total[jnp.maximum(slot_tile(table, THEIRS_AT + first, i), 0)]


def pick(table, first, last, total):
    chunks = last - first
    return pl.pallas_call(
        functools.partial(pick_kernel, first, chunks),
        out_shape=jax.ShapeDtypeStruct((chunks * CAP, BLK, BLK), F32),
        in_specs=[smem_spec(), vmem_spec()],
        out_specs=vmem_spec(),
        compiler_params=params(PICK_MIB),
        cost_estimate=pl.CostEstimate(
            flops=0, bytes_accessed=chunks * CAP * BLK * BLK * 8, transcendentals=0),
    )(table, total)


def code_kernel(at, coded, plain, table, total, other, *refs):
    chunks = coded + plain
    outs, held = refs[:chunks], refs[chunks]
    for m in range(chunks):
        most = jnp.zeros((1, BLK), F32)
        for t in range(CAP):
            i = m * CAP + t
            tile = slot_tile(table, MINE_AT + at, i)
            both = jnp.where(tile >= 0, total[jnp.maximum(tile, 0)] + other[i], 0.0)
            if m >= coded:
                outs[m][t] = both
            else:
                held[t] = both
                most = jnp.maximum(most, jnp.max(jnp.abs(both), axis=0, keepdims=True))
        if m < coded:
            level = jnp.ceil(jnp.log2(jnp.maximum(most, 1e-30)))
            scale = jnp.exp2(TOP - level)
            for t in range(CAP):
                v = held[t] * scale
                v2 = v * v
                v4 = v2 * v2
                outs[m][t * BLK:(t + 1) * BLK, :] = (v4 * v4 * v).astype(BF16)
            outs[m][CAP * BLK:, :] = jnp.broadcast_to(level, (TAIL, BLK)).astype(BF16)


def code(table, first, last, total, other, plain):
    chunks = last - first
    coded = chunks - plain
    return pl.pallas_call(
        functools.partial(code_kernel, first, coded, plain),
        out_shape=[jax.ShapeDtypeStruct((CAP * BLK + TAIL, BLK), BF16)] * coded
        + [jax.ShapeDtypeStruct((CAP, BLK, BLK), F32)] * plain,
        in_specs=[smem_spec(), vmem_spec(), vmem_spec()],
        out_specs=[vmem_spec()] * chunks,
        scratch_shapes=[pltpu.VMEM((CAP, BLK, BLK), F32)],
        compiler_params=params(CODE_MIB),
        cost_estimate=pl.CostEstimate(
            flops=chunks * CAP * BLK * BLK * 8, bytes_accessed=chunks * CAP * BLK * BLK * 10,
            transcendentals=0),
    )(table, total, other)


def sum_kernel(own, *refs):
    arrived, out = refs[:-1], refs[-1]
    scales = []
    for ref in arrived:
        level = ref[CAP * BLK:CAP * BLK + TAIL, :].astype(F32)[0:1, :]
        scales.append(level - TOP)
    for t in range(CAP):
        acc = own[t]
        for ref, scale in zip(arrived, scales):
            y = ref[t * BLK:(t + 1) * BLK, :].astype(F32)
            size = jnp.exp2(jnp.log2(jnp.maximum(jnp.abs(y), 1e-37)) * (1.0 / POWER) + scale)
            size = jnp.where(jnp.abs(y) > 1e-37, size, 0.0)
            acc = acc + jnp.where(y < 0, -size, size)
        out[t] = acc


def total_sum(own, arrived):
    return pl.pallas_call(
        sum_kernel,
        out_shape=jax.ShapeDtypeStruct((CAP, BLK, BLK), F32),
        in_specs=[vmem_spec()] * (1 + len(arrived)),
        out_specs=vmem_spec(),
        compiler_params=params(24),
        cost_estimate=pl.CostEstimate(
            flops=8 * CAP * BLK * BLK * 8, bytes_accessed=8 * CAP * BLK * BLK * 2,
            transcendentals=0),
    )(own, *arrived)


def grad_kernel(ids, has_sum, last, table, *refs):
    count = len(ids)
    blocks, parts = refs[:count], refs[count:count + 8]
    refs = refs[count + 8:]
    before = refs[0] if has_sum else None
    out, weights, total = refs[1 if has_sum else 0:]
    side = table[SIDE_AT]
    core = table[SIDE_AT + 1]
    for k in range(8):
        weights[core if k < 4 else 1 - core, (k % 4) * 512:(k % 4 + 1) * 512, :] = parts[k][...]
    for k, place in enumerate(ids):
        dxh = COLS[place][1]
        first = pl.multiple_of((side if dxh == 0 else 1 - side) * 512, 512)
        for h in range(2):
            row = pl.multiple_of(table[ROW_AT + h * 16 + place] * 256, 256)
            made = lax.dot_general(
                blocks[k][...], weights[h, pl.ds(row, 256), pl.ds(first, 512)],
                (((1,), (1,)), ((), ())), preferred_element_type=F32)
            cols = slice(h * 256, (h + 1) * 256)
            if k > 0:
                made = made + total[:, cols]
            elif has_sum:
                made = made + before[:, cols]
            if k < count - 1:
                total[:, cols] = made
            else:
                out[:, cols] = made.astype(out.dtype)


def grad_sum(table, ids, blocks, parts, before, last):
    count = len(ids)
    has_sum = before is not None
    return pl.pallas_call(
        functools.partial(grad_kernel, tuple(ids), has_sum, last),
        out_shape=jax.ShapeDtypeStruct((512, 512), BF16 if last else F32),
        in_specs=[smem_spec()] + [vmem_spec()] * (count + 8 + has_sum),
        out_specs=vmem_spec(),
        scratch_shapes=[pltpu.VMEM((2, 2048, 1024), BF16), pltpu.VMEM((512, 512), F32)],
        compiler_params=params(GRAD_MIB),
        cost_estimate=pl.CostEstimate(
            flops=2 * 512 ** 3 * count, bytes_accessed=(8 + count) * 1024 * 1024, transcendentals=0),
    )(table, *blocks, *parts, *([before] if has_sum else []))


def body(inputs, grad_out, weight, blocks, owner):
    row = lax.axis_index("row")
    col = lax.axis_index("col")
    core = lax.axis_index("srv")
    x_lo, y = row // 4, row % 4
    z, x_hi = col // 2, col % 2

    sign = 1 - 2 * core

    def ahead(v):
        return lax.ppermute(v, ("col", "srv"), z_shift(1))

    def back(v):
        return lax.ppermute(v, ("col", "srv"), z_shift(-1))

    def across(v):
        return lax.ppermute(v, "col", X_SWAP)

    def around(v):
        return lax.ppermute(v, ("row", "srv"), y_shift(1))

    def to_row(v, dx, dy):
        return lax.ppermute(v, "row", row_shift(dx, dy))

    def to_core(v):
        return lax.ppermute(v, "srv", CORE_SWAP)

    together = lax.optimization_barrier

    listed = blocks[0]
    owners = owner[0]
    live = listed[:, 0] >= 0
    order = jnp.arange(listed.shape[0], dtype=jnp.int32)
    same = owners[:, None] == owners[None, :]
    earlier = order[None, :] < order[:, None]
    rank = jnp.sum((same & earlier & live[None, :]).astype(jnp.int32), axis=1)
    position = jnp.where(live, owners * CAP + rank, -1)
    tile = jnp.where(live, listed[:, 1] * 4 + listed[:, 0] % 4, 0)
    fills = position[None, :] == order[:, None]
    slots = jnp.sum(jnp.where(fills, tile[None, :] + 1, 0), axis=1) - 1

    z_of = (z + sign * np.array([dz for dz, _ in COLS])) % 8
    col_of = z_of * 2 + (x_hi ^ np.array([dxh for _, dxh in COLS]))
    found = []
    for h in range(2):
        turn = np.array([t for t in range(4) for _ in range(2)])
        ids = (x_lo ^ np.array([dx for _ in range(4) for dx in range(2)])) * 4 + (y - (1 - 2 * h) * turn) % 4
        hit = ids[None, :] == z_of[:, None]
        found.append(jnp.sum(jnp.where(hit, np.arange(8)[None, :], 0), axis=1))
    dest = (x_lo ^ np.array([dx for dx, _ in DESTS])) * 4 + (y + np.array([dy for _, dy in DESTS])) % 4
    table = jnp.concatenate([
        v.astype(jnp.int32)
        for v in (col_of, *found, x_hi[None], core[None], dest * 2 + core, dest * 2 + 1 - core, slots)])
    xt = inputs.T

    half = lax.dynamic_slice_in_dim(weight, core * 256, 256, 0)
    far_half, r1, f1, table, xt = together(
        (to_row(half, 1, 0), back(grad_out), ahead(grad_out), table, xt))

    pair = jnp.concatenate([half, far_half], axis=0)
    total = dense(None, table, xt, [grad_out, f1, r1], 0)
    s0, w1, o0, r2, f2, total = together(
        (to_core(pair), around(pair), across(grad_out), back(r1), ahead(f1), total))

    total = dense(total, table, xt, [f2, r2, o0], 3)
    s1, w2, of2, r3, f3, total = together(
        (to_core(w1), around(w1), across(f2), back(r2), ahead(f2), total))

    total = dense(total, table, xt, [f3, r3, of2], 6)
    w3, or2, or1, of1, f4, total = together(
        (around(w2), across(r2), back(o0), ahead(o0), ahead(f3), total))

    total = dense(total, table, xt, [f4, of1, or1, or2], 9)
    s3, s2, of4, or3, of3, total = together(
        (to_core(w3), to_core(w2), across(f4), back(or2), ahead(of2), total))

    total = dense(total, table, xt, [of3, or3, of4], LAST)
    parts = [pair, w1, w2, w3, s0, s1, s2, s3]
    cols = [grad_out, f1, r1, f2, r2, o0, f3, r3, of2, f4, of1, or1, or2, of3, or3, of4]

    other_late = to_core(pick(table, EARLY, 8, total))
    other_early = to_core(pick(table, 0, EARLY, total))
    early = code(table, 0, EARLY, total, other_early, 0)
    late = code(table, EARLY, 8, total, other_late, 1)
    coded = list(early) + list(late[:-1])
    arrived = [to_row(v, dx, dy) for v, (dx, dy) in zip(coded, DESTS)]
    own, grad_table = together((late[-1], table))
    grad_in = grad_sum(grad_table, range(16), cols, parts, None, True)
    *arrived, grad_in = together((*arrived, grad_in))
    pushed = total_sum(own, arrived)
    return grad_in, pushed.reshape(1, CAP, BLK, BLK)


def solution(mesh):
    in_specs = (
        P(("row", "srv"), "col"),
        P(("row", "srv"), "col"),
        P("col", "row"),
        P("col", None, None),
        P("col", None),
    )
    out_specs = (P(("row", "srv"), "col"), P(("row", "srv"), "col", None, None))
    return jax.shard_map(body, mesh=mesh, in_specs=in_specs, out_specs=out_specs, check_vma=False)
```

```python
import functools

import jax
import jax.numpy as jnp
import numpy as np
from jax import lax
from jax.experimental import pallas as pl
from jax.experimental.pallas import tpu as pltpu
from jax.sharding import PartitionSpec as P

BLK = 128
CAP = 8
POWER = 9
TOP = 13.0
TAIL = 16
F32 = jnp.float32
BF16 = jnp.bfloat16

COLS = ((0, 0), (-1, 0), (1, 0), (-2, 0), (2, 0), (0, 1), (-3, 0), (3, 0), (-2, 1),
        (-4, 0), (-1, 1), (1, 1), (2, 1), (-3, 1), (3, 1), (-4, 1))
LAST = 13
DESTS = ((1, 2), (1, 1), (1, 3), (1, 0), (0, 2), (0, 1), (0, 3), (0, 0))
EARLY = 2
DENSE_MIB = PICK_MIB = CODE_MIB = GRAD_MIB = 20
COL_AT, ROW_AT, SIDE_AT, MINE_AT, THEIRS_AT, SLOT_AT = 0, 16, 48, 50, 58, 66


def z_shift(d):
    return [((z * 2 + h) * 2 + c, (((z + (1 - 2 * c) * d) % 8) * 2 + h) * 2 + c)
            for z in range(8) for h in range(2) for c in range(2)]


def y_shift(d):
    return [((l * 4 + y) * 2 + c, (l * 4 + (y + (1 - 2 * c) * d) % 4) * 2 + c)
            for l in range(2) for y in range(4) for c in range(2)]


def row_shift(dx, dy):
    return [(l * 4 + y, (l ^ dx) * 4 + (y + dy) % 4) for l in range(2) for y in range(4)]


X_SWAP = [(z * 2 + h, z * 2 + 1 - h) for z in range(8) for h in range(2)]
CORE_SWAP = [(0, 1), (1, 0)]


def hbm_spec():
    return pl.BlockSpec(memory_space=pltpu.HBM)


def smem_spec():
    return pl.BlockSpec(memory_space=pltpu.SMEM)


def vmem_spec():
    return pl.BlockSpec(memory_space=pltpu.VMEM)


def params(mib):
    return pltpu.CompilerParams(vmem_limit_bytes=mib * 1024 * 1024)


def dense_kernel(count, place, first, table, xt_ref, *refs):
    blocks = refs[:count]
    out = refs[count + (0 if first else 1)]
    for j in range(count):
        acc = jnp.dot(xt_ref[...], blocks[j][...], preferred_element_type=F32)
        at = table[COL_AT + place + j] * 16
        for cc in range(4):
            for rb in range(4):
                out[at + cc * 4 + rb] = acc[rb * BLK:(rb + 1) * BLK, cc * BLK:(cc + 1) * BLK]


def dense(total, table, xt, blocks, place):
    count = len(blocks)
    first = total is None
    args = [table, xt, *blocks] + ([] if first else [total])
    return pl.pallas_call(
        functools.partial(dense_kernel, count, place, first),
        out_shape=jax.ShapeDtypeStruct((256, BLK, BLK), F32),
        in_specs=[smem_spec(), vmem_spec()] + [vmem_spec()] * count + ([] if first else [vmem_spec()]),
        out_specs=vmem_spec(),
        input_output_aliases={} if first else {2 + count: 0},
        compiler_params=params(DENSE_MIB),
        cost_estimate=pl.CostEstimate(
            flops=count * 2 * 512 ** 3, bytes_accessed=count * 3 * 512 * 1024, transcendentals=0),
    )(*args)


def slot_tile(table, owner_at, i):
    return table[SLOT_AT + table[owner_at + i // CAP] * CAP + i % CAP]


def pick_kernel(first, chunks, table, total, out):
    for i in range(chunks * CAP):
        out[i] = total[jnp.maximum(slot_tile(table, THEIRS_AT + first, i), 0)]


def pick(table, first, last, total):
    chunks = last - first
    return pl.pallas_call(
        functools.partial(pick_kernel, first, chunks),
        out_shape=jax.ShapeDtypeStruct((chunks * CAP, BLK, BLK), F32),
        in_specs=[smem_spec(), vmem_spec()],
        out_specs=vmem_spec(),
        compiler_params=params(PICK_MIB),
        cost_estimate=pl.CostEstimate(
            flops=0, bytes_accessed=chunks * CAP * BLK * BLK * 8, transcendentals=0),
    )(table, total)


def code_kernel(at, coded, plain, table, total, other, *refs):
    chunks = coded + plain
    outs, held = refs[:chunks], refs[chunks]
    for m in range(chunks):
        most = jnp.zeros((1, BLK), F32)
        for t in range(CAP):
            i = m * CAP + t
            tile = slot_tile(table, MINE_AT + at, i)
            both = jnp.where(tile >= 0, total[jnp.maximum(tile, 0)] + other[i], 0.0)
            if m >= coded:
                outs[m][t] = both
            else:
                held[t] = both
                most = jnp.maximum(most, jnp.max(jnp.abs(both), axis=0, keepdims=True))
        if m < coded:
            level = jnp.ceil(jnp.log2(jnp.maximum(most, 1e-30)))
            scale = jnp.exp2(TOP - level)
            for t in range(CAP):
                v = held[t] * scale
                v2 = v * v
                v4 = v2 * v2
                outs[m][t * BLK:(t + 1) * BLK, :] = (v4 * v4 * v).astype(BF16)
            outs[m][CAP * BLK:, :] = jnp.broadcast_to(level, (TAIL, BLK)).astype(BF16)


def code(table, first, last, total, other, plain):
    chunks = last - first
    coded = chunks - plain
    return pl.pallas_call(
        functools.partial(code_kernel, first, coded, plain),
        out_shape=[jax.ShapeDtypeStruct((CAP * BLK + TAIL, BLK), BF16)] * coded
        + [jax.ShapeDtypeStruct((CAP, BLK, BLK), F32)] * plain,
        in_specs=[smem_spec(), vmem_spec(), vmem_spec()],
        out_specs=[vmem_spec()] * chunks,
        scratch_shapes=[pltpu.VMEM((CAP, BLK, BLK), F32)],
        compiler_params=params(CODE_MIB),
        cost_estimate=pl.CostEstimate(
            flops=chunks * CAP * BLK * BLK * 8, bytes_accessed=chunks * CAP * BLK * BLK * 10,
            transcendentals=0),
    )(table, total, other)


def sum_kernel(before, *refs):
    arrived, out = refs[:-1], refs[-1]
    scales = []
    for ref in arrived:
        level = ref[CAP * BLK:CAP * BLK + TAIL, :].astype(F32)[0:1, :]
        scales.append(level - TOP)
    for t in range(CAP):
        acc = before[t]
        for ref, scale in zip(arrived, scales):
            y = ref[t * BLK:(t + 1) * BLK, :].astype(F32)
            size = jnp.exp2(jnp.log2(jnp.maximum(jnp.abs(y), 1e-37)) * (1.0 / POWER) + scale)
            size = jnp.where(jnp.abs(y) > 1e-37, size, 0.0)
            acc = acc + jnp.where(y < 0, -size, size)
        out[t] = acc


def add_coded(before, arrived):
    count = len(arrived)
    return pl.pallas_call(
        sum_kernel,
        out_shape=jax.ShapeDtypeStruct((CAP, BLK, BLK), F32),
        in_specs=[vmem_spec()] * (1 + count),
        out_specs=vmem_spec(),
        compiler_params=params(20),
        cost_estimate=pl.CostEstimate(
            flops=count * CAP * BLK * BLK * 8, bytes_accessed=count * CAP * BLK * BLK * 2,
            transcendentals=0),
    )(before, *arrived)


def grad_kernel(ids, has_sum, last, table, *refs):
    count = len(ids)
    blocks, parts = refs[:count], refs[count:count + 4]
    refs = refs[count + 4:]
    before = refs[0] if has_sum else None
    out, weights, total = refs[1 if has_sum else 0:]
    side = table[SIDE_AT]
    core = table[SIDE_AT + 1]
    for k in range(4):
        rows = slice(0, 1536) if k % 2 == 0 else slice(1536, 2048)
        weights[core if k < 2 else 1 - core, rows, :] = parts[k][...]
    for k, place in enumerate(ids):
        dxh = COLS[place][1]
        first = pl.multiple_of((side if dxh == 0 else 1 - side) * 512, 512)
        for h in range(2):
            row = pl.multiple_of(table[ROW_AT + h * 16 + place] * 256, 256)
            made = lax.dot_general(
                blocks[k][...], weights[h, pl.ds(row, 256), pl.ds(first, 512)],
                (((1,), (1,)), ((), ())), preferred_element_type=F32)
            cols = slice(h * 256, (h + 1) * 256)
            if k > 0:
                made = made + total[:, cols]
            elif has_sum:
                made = made + before[:, cols]
            if k < count - 1:
                total[:, cols] = made
            else:
                out[:, cols] = made.astype(out.dtype)


def grad_sum(table, ids, blocks, parts, before, last):
    count = len(ids)
    has_sum = before is not None
    return pl.pallas_call(
        functools.partial(grad_kernel, tuple(ids), has_sum, last),
        out_shape=jax.ShapeDtypeStruct((512, 512), BF16 if last else F32),
        in_specs=[smem_spec()] + [vmem_spec()] * (count + 4 + has_sum),
        out_specs=vmem_spec(),
        scratch_shapes=[pltpu.VMEM((2, 2048, 1024), BF16), pltpu.VMEM((512, 512), F32)],
        compiler_params=params(GRAD_MIB),
        cost_estimate=pl.CostEstimate(
            flops=2 * 512 ** 3 * count, bytes_accessed=(8 + count) * 1024 * 1024, transcendentals=0),
    )(table, *blocks, *parts, *([before] if has_sum else []))


def join_kernel(*refs):
    first = 0
    for part in refs[:-1]:
        refs[-1][first:first + part.shape[0], :] = part[...]
        first += part.shape[0]


def join(parts):
    rows = sum(part.shape[0] for part in parts)
    return pl.pallas_call(
        join_kernel,
        out_shape=jax.ShapeDtypeStruct((rows, parts[0].shape[1]), parts[0].dtype),
        in_specs=[vmem_spec()] * len(parts),
        out_specs=vmem_spec(),
        compiler_params=params(20),
        cost_estimate=pl.CostEstimate(
            flops=0, bytes_accessed=4 * rows * parts[0].shape[1], transcendentals=0),
    )(*parts)


def body(inputs, grad_out, weight, blocks, owner):
    row = lax.axis_index("row")
    col = lax.axis_index("col")
    core = lax.axis_index("srv")
    x_lo, y = row // 4, row % 4
    z, x_hi = col // 2, col % 2

    sign = 1 - 2 * core

    def ahead(v):
        return lax.ppermute(v, ("col", "srv"), z_shift(1))

    def back(v):
        return lax.ppermute(v, ("col", "srv"), z_shift(-1))

    def across(v):
        return lax.ppermute(v, "col", X_SWAP)

    def around(v):
        return lax.ppermute(v, ("row", "srv"), y_shift(1))

    def to_row(v, dx, dy):
        return lax.ppermute(v, "row", row_shift(dx, dy))

    def to_core(v):
        return lax.ppermute(v, "srv", CORE_SWAP)

    together = lax.optimization_barrier

    listed = blocks[0]
    owners = owner[0]
    live = listed[:, 0] >= 0
    order = jnp.arange(listed.shape[0], dtype=jnp.int32)
    same = owners[:, None] == owners[None, :]
    earlier = order[None, :] < order[:, None]
    rank = jnp.sum((same & earlier & live[None, :]).astype(jnp.int32), axis=1)
    position = jnp.where(live, owners * CAP + rank, -1)
    tile = jnp.where(live, listed[:, 1] * 4 + listed[:, 0] % 4, 0)
    fills = position[None, :] == order[:, None]
    slots = jnp.sum(jnp.where(fills, tile[None, :] + 1, 0), axis=1) - 1

    z_of = (z + sign * np.array([dz for dz, _ in COLS])) % 8
    col_of = z_of * 2 + (x_hi ^ np.array([dxh for _, dxh in COLS]))
    found = []
    for h in range(2):
        turn = np.array([t for t in range(4) for _ in range(2)])
        ids = (x_lo ^ np.array([dx for _ in range(4) for dx in range(2)])) * 4 + (y - (1 - 2 * h) * turn) % 4
        hit = ids[None, :] == z_of[:, None]
        found.append(jnp.sum(jnp.where(hit, np.arange(8)[None, :], 0), axis=1))
    dest = (x_lo ^ np.array([dx for dx, _ in DESTS])) * 4 + (y + np.array([dy for _, dy in DESTS])) % 4
    table = jnp.concatenate([
        v.astype(jnp.int32)
        for v in (col_of, *found, x_hi[None], core[None], dest * 2 + core, dest * 2 + 1 - core, slots)])
    xt = inputs.T

    half = lax.dynamic_slice_in_dim(weight, core * 256, 256, 0)
    o0 = across(grad_out)
    r1, f1, table, xt, half = together((back(grad_out), ahead(grad_out), table, xt, half))

    total = dense(None, table, xt, [grad_out, f1, r1], 0)
    o0, far_half, r2, f2, total = together((o0, to_row(half, 1, 0), back(r1), ahead(f1), total))

    pair = jnp.concatenate([half, far_half], axis=0)
    total = dense(total, table, xt, [f2, r2, o0], 3)
    w1, of2, of1, r3, f3, total = together(
        (around(pair), across(f2), ahead(o0), back(r2), ahead(f2), total))

    total = dense(total, table, xt, [f3, r3, of2], 6)
    w2, or2, or1, f4, total = together((around(w1), across(r2), back(o0), ahead(f3), total))

    total = dense(total, table, xt, [f4, of1, or1, or2], 9)
    mine = join([pair, w1, w2])
    w3, theirs, of4, or3, of3, total = together(
        (around(w2), to_core(mine), across(f4), back(or2), ahead(of2), total))

    total = dense(total, table, xt, [of3, or3, of4], LAST)
    cols = [grad_out, f1, r1, f2, r2, o0, f3, r3, of2, f4, of1, or1, or2, of3, or3, of4]

    other_early = to_core(pick(table, 0, EARLY, total))
    early = code(table, 0, EARLY, total, other_early, 0)
    *early, w3, late_table = together((*early, w3, table))
    other_late = to_core(pick(late_table, EARLY, 8, total))
    parts = [mine, w3, theirs, to_core(w3)]
    late = code(late_table, EARLY, 8, total, other_late, 1)
    coded = list(early) + list(late[:-1])
    arrived = [to_row(v, dx, dy) for v, (dx, dy) in zip(coded, DESTS)]
    own, grad_table = together((late[-1], late_table))
    grad_in = grad_sum(grad_table, range(16), cols, parts, None, True)
    first, second, grad_in = together((arrived[0], arrived[1], grad_in))
    pushed = add_coded(own, [first, second, arrived[2], arrived[3]])
    pushed = add_coded(pushed, arrived[4:])
    return grad_in, pushed.reshape(1, CAP, BLK, BLK)


def solution(mesh):
    in_specs = (
        P(("row", "srv"), "col"),
        P(("row", "srv"), "col"),
        P("col", "row"),
        P("col", None, None),
        P("col", None),
    )
    out_specs = (P(("row", "srv"), "col"), P(("row", "srv"), "col", None, None))
    return jax.shard_map(body, mesh=mesh, in_specs=in_specs, out_specs=out_specs, check_vma=False)
```

```python
import functools

import jax
import jax.numpy as jnp
import numpy as np
from jax import lax
from jax.experimental import pallas as pl
from jax.experimental.pallas import tpu as pltpu
from jax.sharding import PartitionSpec as P

BLK = 128
CAP = 8
POWER = 9
TOP = 13.0
TAIL = 16
F32 = jnp.float32
BF16 = jnp.bfloat16

COLS = ((0, 0), (-1, 0), (1, 0), (-2, 0), (2, 0), (0, 1), (-3, 0), (3, 0), (-2, 1),
        (-4, 0), (-1, 1), (1, 1), (2, 1), (-3, 1), (3, 1), (-4, 1))
LAST = 13
DESTS = ((1, 2), (1, 1), (1, 3), (1, 0), (0, 2), (0, 1), (0, 3), (0, 0))
EARLY = 2
PHASE_FLOPS = 30 * 10 ** 9
DENSE_MIB = PICK_MIB = CODE_MIB = GRAD_MIB = 10
COL_AT, ROW_AT, SIDE_AT, MINE_AT, THEIRS_AT, SLOT_AT = 0, 16, 48, 50, 58, 66


def z_shift(d):
    return [((z * 2 + h) * 2 + c, (((z + (1 - 2 * c) * d) % 8) * 2 + h) * 2 + c)
            for z in range(8) for h in range(2) for c in range(2)]


def y_shift(d):
    return [((l * 4 + y) * 2 + c, (l * 4 + (y + (1 - 2 * c) * d) % 4) * 2 + c)
            for l in range(2) for y in range(4) for c in range(2)]


def row_shift(dx, dy):
    return [(l * 4 + y, (l ^ dx) * 4 + (y + dy) % 4) for l in range(2) for y in range(4)]


X_SWAP = [(z * 2 + h, z * 2 + 1 - h) for z in range(8) for h in range(2)]
CORE_SWAP = [(0, 1), (1, 0)]


def hbm_spec():
    return pl.BlockSpec(memory_space=pltpu.HBM)


def smem_spec():
    return pl.BlockSpec(memory_space=pltpu.SMEM)


def vmem_spec():
    return pl.BlockSpec(memory_space=pltpu.VMEM)


def params(mib):
    return pltpu.CompilerParams(vmem_limit_bytes=mib * 1024 * 1024)


def dense_kernel(count, place, first, table, xt_ref, *refs):
    blocks = refs[:count]
    out = refs[count + (0 if first else 1)]
    for j in range(count):
        acc = jnp.dot(xt_ref[...], blocks[j][...], preferred_element_type=F32)
        at = table[COL_AT + place + j] * 16
        for cc in range(4):
            for rb in range(4):
                out[at + cc * 4 + rb] = acc[rb * BLK:(rb + 1) * BLK, cc * BLK:(cc + 1) * BLK]


def dense(total, table, xt, blocks, place):
    count = len(blocks)
    first = total is None
    args = [table, xt, *blocks] + ([] if first else [total])
    return pl.pallas_call(
        functools.partial(dense_kernel, count, place, first),
        out_shape=jax.ShapeDtypeStruct((256, BLK, BLK), F32),
        in_specs=[smem_spec(), vmem_spec()] + [vmem_spec()] * count + ([] if first else [vmem_spec()]),
        out_specs=vmem_spec(),
        input_output_aliases={} if first else {2 + count: 0},
        compiler_params=params(DENSE_MIB),
        cost_estimate=pl.CostEstimate(
            flops=PHASE_FLOPS, bytes_accessed=count * 3 * 512 * 1024, transcendentals=0),
    )(*args)


def slot_tile(table, owner_at, i):
    return table[SLOT_AT + table[owner_at + i // CAP] * CAP + i % CAP]


def pick_kernel(first, chunks, table, total, out):
    for i in range(chunks * CAP):
        out[i] = total[jnp.maximum(slot_tile(table, THEIRS_AT + first, i), 0)]


def pick(table, first, last, total):
    chunks = last - first
    return pl.pallas_call(
        functools.partial(pick_kernel, first, chunks),
        out_shape=jax.ShapeDtypeStruct((chunks * CAP, BLK, BLK), F32),
        in_specs=[smem_spec(), vmem_spec()],
        out_specs=vmem_spec(),
        compiler_params=params(PICK_MIB),
        cost_estimate=pl.CostEstimate(
            flops=0, bytes_accessed=chunks * CAP * BLK * BLK * 8, transcendentals=0),
    )(table, total)


def code_kernel(at, coded, plain, table, total, other, *refs):
    chunks = coded + plain
    outs, held = refs[:chunks], refs[chunks]
    for m in range(chunks):
        most = jnp.zeros((1, BLK), F32)
        for t in range(CAP):
            i = m * CAP + t
            tile = slot_tile(table, MINE_AT + at, i)
            both = jnp.where(tile >= 0, total[jnp.maximum(tile, 0)] + other[i], 0.0)
            if m >= coded:
                outs[m][t] = both
            else:
                held[t] = both
                most = jnp.maximum(most, jnp.max(jnp.abs(both), axis=0, keepdims=True))
        if m < coded:
            level = jnp.ceil(jnp.log2(jnp.maximum(most, 1e-30)))
            scale = jnp.exp2(TOP - level)
            for t in range(CAP):
                v = held[t] * scale
                v2 = v * v
                v4 = v2 * v2
                outs[m][t * BLK:(t + 1) * BLK, :] = (v4 * v4 * v).astype(BF16)
            outs[m][CAP * BLK:, :] = jnp.broadcast_to(level, (TAIL, BLK)).astype(BF16)


def code(table, first, last, total, other, plain):
    chunks = last - first
    coded = chunks - plain
    return pl.pallas_call(
        functools.partial(code_kernel, first, coded, plain),
        out_shape=[jax.ShapeDtypeStruct((CAP * BLK + TAIL, BLK), BF16)] * coded
        + [jax.ShapeDtypeStruct((CAP, BLK, BLK), F32)] * plain,
        in_specs=[smem_spec(), vmem_spec(), vmem_spec()],
        out_specs=[vmem_spec()] * chunks,
        scratch_shapes=[pltpu.VMEM((CAP, BLK, BLK), F32)],
        compiler_params=params(CODE_MIB),
        cost_estimate=pl.CostEstimate(
            flops=chunks * CAP * BLK * BLK * 8, bytes_accessed=chunks * CAP * BLK * BLK * 10,
            transcendentals=0),
    )(table, total, other)


def sum_kernel(before, *refs):
    arrived, out = refs[:-1], refs[-1]
    scales = []
    for ref in arrived:
        level = ref[CAP * BLK:CAP * BLK + TAIL, :].astype(F32)[0:1, :]
        scales.append(level - TOP)
    for t in range(CAP):
        acc = before[t]
        for ref, scale in zip(arrived, scales):
            y = ref[t * BLK:(t + 1) * BLK, :].astype(F32)
            size = jnp.exp2(jnp.log2(jnp.maximum(jnp.abs(y), 1e-37)) * (1.0 / POWER) + scale)
            size = jnp.where(jnp.abs(y) > 1e-37, size, 0.0)
            acc = acc + jnp.where(y < 0, -size, size)
        out[t] = acc


def add_coded(before, arrived):
    count = len(arrived)
    return pl.pallas_call(
        sum_kernel,
        out_shape=jax.ShapeDtypeStruct((CAP, BLK, BLK), F32),
        in_specs=[vmem_spec()] * (1 + count),
        out_specs=vmem_spec(),
        compiler_params=params(10),
        cost_estimate=pl.CostEstimate(
            flops=count * CAP * BLK * BLK * 8, bytes_accessed=count * CAP * BLK * BLK * 2,
            transcendentals=0),
    )(before, *arrived)


def grad_kernel(ids, table, *refs):
    count = len(ids)
    blocks, mine, theirs, out, total = refs[:count], *refs[count:]
    side = table[SIDE_AT]
    core = table[SIDE_AT + 1]
    for k, place in enumerate(ids):
        dxh = COLS[place][1]
        first = pl.multiple_of((side if dxh == 0 else 1 - side) * 512, 512)
        for part, half in enumerate((core, 1 - core)):
            rows = pl.multiple_of(table[ROW_AT + half * 16 + place] * 256, 256)
            weights = (mine, theirs)[part][pl.ds(rows, 256), pl.ds(first, 512)]
            made = lax.dot_general(
                blocks[k][...], weights, (((1,), (1,)), ((), ())), preferred_element_type=F32)
            if k > 0:
                made = made + total[part]
            if k < count - 1:
                total[part] = made
            else:
                out[:, pl.ds(pl.multiple_of(half * 256, 256), 256)] = made.astype(out.dtype)


def grad_sum(table, ids, blocks, parts):
    count = len(ids)
    return pl.pallas_call(
        functools.partial(grad_kernel, tuple(ids)),
        out_shape=jax.ShapeDtypeStruct((512, 512), BF16),
        in_specs=[smem_spec()] + [vmem_spec()] * (count + 2),
        out_specs=vmem_spec(),
        scratch_shapes=[pltpu.VMEM((2, 512, 256), F32)],
        compiler_params=params(GRAD_MIB),
        cost_estimate=pl.CostEstimate(
            flops=2 * 512 ** 3 * count, bytes_accessed=(8 + count) * 1024 * 1024, transcendentals=0),
    )(table, *blocks, *parts)


def join_kernel(*refs):
    first = 0
    for part in refs[:-1]:
        refs[-1][first:first + part.shape[0], :] = part[...]
        first += part.shape[0]


def join(parts):
    rows = sum(part.shape[0] for part in parts)
    return pl.pallas_call(
        join_kernel,
        out_shape=jax.ShapeDtypeStruct((rows, parts[0].shape[1]), parts[0].dtype),
        in_specs=[vmem_spec()] * len(parts),
        out_specs=vmem_spec(),
        compiler_params=params(10),
        cost_estimate=pl.CostEstimate(
            flops=0, bytes_accessed=0, transcendentals=0),
    )(*parts)


def body(inputs, grad_out, weight, blocks, owner):
    row = lax.axis_index("row")
    col = lax.axis_index("col")
    core = lax.axis_index("srv")
    x_lo, y = row // 4, row % 4
    z, x_hi = col // 2, col % 2

    sign = 1 - 2 * core

    def ahead(v):
        return lax.ppermute(v, ("col", "srv"), z_shift(1))

    def back(v):
        return lax.ppermute(v, ("col", "srv"), z_shift(-1))

    def across(v):
        return lax.ppermute(v, "col", X_SWAP)

    def around(v):
        return lax.ppermute(v, ("row", "srv"), y_shift(1))

    def to_row(v, dx, dy):
        return lax.ppermute(v, "row", row_shift(dx, dy))

    def to_core(v):
        return lax.ppermute(v, "srv", CORE_SWAP)

    together = lax.optimization_barrier

    listed = blocks[0]
    owners = owner[0]
    live = listed[:, 0] >= 0
    order = jnp.arange(listed.shape[0], dtype=jnp.int32)
    same = owners[:, None] == owners[None, :]
    earlier = order[None, :] < order[:, None]
    rank = jnp.sum((same & earlier & live[None, :]).astype(jnp.int32), axis=1)
    position = jnp.where(live, owners * CAP + rank, -1)
    tile = jnp.where(live, listed[:, 1] * 4 + listed[:, 0] % 4, 0)
    fills = position[None, :] == order[:, None]
    slots = jnp.sum(jnp.where(fills, tile[None, :] + 1, 0), axis=1) - 1

    z_of = (z + sign * np.array([dz for dz, _ in COLS])) % 8
    col_of = z_of * 2 + (x_hi ^ np.array([dxh for _, dxh in COLS]))
    found = []
    for h in range(2):
        turn = np.array([t for t in range(4) for _ in range(2)])
        ids = (x_lo ^ np.array([dx for _ in range(4) for dx in range(2)])) * 4 + (y - (1 - 2 * h) * turn) % 4
        hit = ids[None, :] == z_of[:, None]
        found.append(jnp.sum(jnp.where(hit, np.arange(8)[None, :], 0), axis=1))
    dest = (x_lo ^ np.array([dx for dx, _ in DESTS])) * 4 + (y + np.array([dy for _, dy in DESTS])) % 4
    table = jnp.concatenate([
        v.astype(jnp.int32)
        for v in (col_of, *found, x_hi[None], core[None], dest * 2 + core, dest * 2 + 1 - core, slots)])
    xt = inputs.T

    half = lax.dynamic_slice_in_dim(weight, core * 256, 256, 0)
    far_half = to_row(half, 1, 0)
    r1, f1, own, table, xt = together((back(grad_out), ahead(grad_out), grad_out, table, xt))

    near_half, far_half, own, now = together((half, far_half, own, table))
    o0 = across(own)
    pair = join([near_half, far_half])
    w1 = around(pair)
    total = dense(None, now, xt, [grad_out, f1, r1], 0)
    o0, r2, f2, total = together((o0, back(r1), ahead(f1), total))

    w1, now = together((w1, table))
    w2 = around(w1)
    total = dense(total, now, xt, [f2, r2, o0], 3)
    of2, of1, r3, f3, total = together((across(f2), ahead(o0), back(r2), ahead(f2), total))

    w2, now = together((w2, table))
    w3 = around(w2)
    total = dense(total, now, xt, [f3, r3, of2], 6)
    or2, or1, f4, total = together((across(r2), back(o0), ahead(f3), total))

    w3, now = together((w3, table))
    mine = join([pair, w1, w2, w3])
    theirs = to_core(mine)
    total = dense(total, now, xt, [f4, of1, or1, or2], 9)
    of4, or3, of3, total = together((across(f4), back(or2), ahead(of2), total))

    total = dense(total, table, xt, [of3, or3, of4], LAST)
    cols = [grad_out, f1, r1, f2, r2, o0, f3, r3, of2, f4, of1, or1, or2, of3, or3, of4]

    other_early = to_core(pick(table, 0, EARLY, total))
    early = code(table, 0, EARLY, total, other_early, 0)
    *early, theirs, late_table = together((*early, theirs, table))
    other_late = to_core(pick(late_table, EARLY, 8, total))
    parts = [mine, theirs]
    late = code(late_table, EARLY, 8, total, other_late, 1)
    coded = list(early) + list(late[:-1])
    arrived = [to_row(v, dx, dy) for v, (dx, dy) in zip(coded, DESTS)]
    own, grad_table = together((late[-1], late_table))
    grad_in = grad_sum(grad_table, range(16), cols, parts)
    first, second, grad_in = together((arrived[0], arrived[1], grad_in))
    pushed = add_coded(own, [first, second, arrived[2], arrived[3]])
    pushed = add_coded(pushed, arrived[4:])
    return grad_in, pushed.reshape(1, CAP, BLK, BLK)


def solution(mesh):
    in_specs = (
        P(("row", "srv"), "col"),
        P(("row", "srv"), "col"),
        P("col", "row"),
        P("col", None, None),
        P("col", None),
    )
    out_specs = (P(("row", "srv"), "col"), P(("row", "srv"), "col", None, None))
    return jax.shard_map(body, mesh=mesh, in_specs=in_specs, out_specs=out_specs, check_vma=False)
```

```python
import functools

import jax
import jax.numpy as jnp
import numpy as np
from jax import lax
from jax.experimental import pallas as pl
from jax.experimental.pallas import tpu as pltpu
from jax.sharding import PartitionSpec as P

BLK = 128
CAP = 8
POWER = 9
TOP = 13.0
TAIL = 16
F32 = jnp.float32
BF16 = jnp.bfloat16

COLS = ((0, 0), (-1, 0), (1, 0), (-2, 0), (2, 0), (0, 1), (-3, 0), (3, 0), (-2, 1),
        (-4, 0), (-1, 1), (1, 1), (2, 1), (-3, 1), (3, 1), (-4, 1))
LAST = 13
DESTS = ((1, 2), (1, 1), (1, 3), (0, 1), (0, 3), (1, 0), (0, 2), (0, 0))
EARLY = 3
DENSE_MIB = PICK_MIB = CODE_MIB = GRAD_MIB = 10
PHASE_FLOPS = 30 * 10 ** 9
DENSE_MIB = PICK_MIB = CODE_MIB = GRAD_MIB = 10
COL_AT, ROW_AT, SIDE_AT, MINE_AT, THEIRS_AT, SLOT_AT = 0, 16, 48, 50, 58, 66


def z_shift(d):
    return [((z * 2 + h) * 2 + c, (((z + (1 - 2 * c) * d) % 8) * 2 + h) * 2 + c)
            for z in range(8) for h in range(2) for c in range(2)]


def y_shift(d):
    return [((l * 4 + y) * 2 + c, (l * 4 + (y + (1 - 2 * c) * d) % 4) * 2 + c)
            for l in range(2) for y in range(4) for c in range(2)]


def row_shift(dx, dy):
    return [(l * 4 + y, (l ^ dx) * 4 + (y + dy) % 4) for l in range(2) for y in range(4)]


X_SWAP = [(z * 2 + h, z * 2 + 1 - h) for z in range(8) for h in range(2)]
CORE_SWAP = [(0, 1), (1, 0)]


def hbm_spec():
    return pl.BlockSpec(memory_space=pltpu.HBM)


def smem_spec():
    return pl.BlockSpec(memory_space=pltpu.SMEM)


def vmem_spec():
    return pl.BlockSpec(memory_space=pltpu.VMEM)


def params(mib):
    return pltpu.CompilerParams(vmem_limit_bytes=mib * 1024 * 1024)


def dense_kernel(count, place, first, table, xt_ref, *refs):
    blocks = refs[:count]
    out = refs[count + (0 if first else 1)]
    for j in range(count):
        acc = jnp.dot(xt_ref[...], blocks[j][...], preferred_element_type=F32)
        at = table[COL_AT + place + j] * 16
        for cc in range(4):
            for rb in range(4):
                out[at + cc * 4 + rb] = acc[rb * BLK:(rb + 1) * BLK, cc * BLK:(cc + 1) * BLK]


def dense(total, table, xt, blocks, place):
    count = len(blocks)
    first = total is None
    args = [table, xt, *blocks] + ([] if first else [total])
    return pl.pallas_call(
        functools.partial(dense_kernel, count, place, first),
        out_shape=jax.ShapeDtypeStruct((256, BLK, BLK), F32),
        in_specs=[smem_spec(), vmem_spec()] + [vmem_spec()] * count + ([] if first else [vmem_spec()]),
        out_specs=vmem_spec(),
        input_output_aliases={} if first else {2 + count: 0},
        compiler_params=params(DENSE_MIB),
        cost_estimate=pl.CostEstimate(
            flops=PHASE_FLOPS, bytes_accessed=count * 3 * 512 * 1024, transcendentals=0),
    )(*args)


def slot_tile(table, owner_at, i):
    return table[SLOT_AT + table[owner_at + i // CAP] * CAP + i % CAP]


def pick_kernel(first, chunks, table, total, out):
    for i in range(chunks * CAP):
        out[i] = total[jnp.maximum(slot_tile(table, THEIRS_AT + first, i), 0)]


def pick(table, first, last, total):
    chunks = last - first
    return pl.pallas_call(
        functools.partial(pick_kernel, first, chunks),
        out_shape=jax.ShapeDtypeStruct((chunks * CAP, BLK, BLK), F32),
        in_specs=[smem_spec(), vmem_spec()],
        out_specs=vmem_spec(),
        compiler_params=params(PICK_MIB),
        cost_estimate=pl.CostEstimate(
            flops=0, bytes_accessed=chunks * CAP * BLK * BLK * 8, transcendentals=0),
    )(table, total)


def encode(held, most, out):
    level = jnp.ceil(jnp.log2(jnp.maximum(most, 1e-30)))
    scale = jnp.exp2(TOP - level)
    for t in range(CAP):
        v = held[t] * scale
        v2 = v * v
        v4 = v2 * v2
        out[t * BLK:(t + 1) * BLK, :] = (v4 * v4 * v).astype(BF16)
    out[CAP * BLK:, :] = jnp.broadcast_to(level, (TAIL, BLK)).astype(BF16)


def scale_of(ref):
    return ref[CAP * BLK:CAP * BLK + TAIL, :].astype(F32)[0:1, :] - TOP


def decode(ref, t, scale):
    y = ref[t * BLK:(t + 1) * BLK, :].astype(F32)
    size = jnp.exp2(jnp.log2(jnp.maximum(jnp.abs(y), 1e-37)) * (1.0 / POWER) + scale)
    size = jnp.where(jnp.abs(y) > 1e-37, size, 0.0)
    return jnp.where(y < 0, -size, size)


def largest(most, tile):
    return jnp.maximum(most, jnp.max(jnp.abs(tile), axis=0, keepdims=True))


def code_kernel(at, coded, plain, table, total, other, *refs):
    chunks = coded + plain
    outs, held = refs[:chunks], refs[chunks]
    for m in range(chunks):
        most = jnp.zeros((1, BLK), F32)
        for t in range(CAP):
            i = m * CAP + t
            tile = slot_tile(table, MINE_AT + at, i)
            both = jnp.where(tile >= 0, total[jnp.maximum(tile, 0)] + other[i], 0.0)
            if m >= coded:
                outs[m][t] = both
            else:
                held[t] = both
                most = largest(most, both)
        if m < coded:
            encode(held, most, outs[m])


def code(table, first, last, total, other, plain):
    chunks = last - first
    coded = chunks - plain
    return pl.pallas_call(
        functools.partial(code_kernel, first, coded, plain),
        out_shape=[jax.ShapeDtypeStruct((CAP * BLK + TAIL, BLK), BF16)] * coded
        + [jax.ShapeDtypeStruct((CAP, BLK, BLK), F32)] * plain,
        in_specs=[smem_spec(), vmem_spec(), vmem_spec()],
        out_specs=[vmem_spec()] * chunks,
        scratch_shapes=[pltpu.VMEM((CAP, BLK, BLK), F32)],
        compiler_params=params(CODE_MIB),
        cost_estimate=pl.CostEstimate(
            flops=chunks * CAP * BLK * BLK * 8, bytes_accessed=chunks * CAP * BLK * BLK * 10,
            transcendentals=0),
    )(table, total, other)


def relay_kernel(counts, *refs):
    outs, held = refs[-1 - len(counts):-1], refs[-1]
    at = 0
    for m, count in enumerate(counts):
        before, arrived = refs[at], refs[at + 1:at + 1 + count]
        at += 1 + count
        scales = [scale_of(ref) for ref in arrived]
        most = jnp.zeros((1, BLK), F32)
        for t in range(CAP):
            acc = before[t]
            for ref, scale in zip(arrived, scales):
                acc = acc + decode(ref, t, scale)
            held[t] = acc
            most = largest(most, acc)
        encode(held, most, outs[m])


def relay(groups):
    counts = tuple(len(arrived) for _, arrived in groups)
    args = [v for before, arrived in groups for v in (before, *arrived)]
    return pl.pallas_call(
        functools.partial(relay_kernel, counts),
        out_shape=[jax.ShapeDtypeStruct((CAP * BLK + TAIL, BLK), BF16)] * len(counts),
        in_specs=[vmem_spec()] * len(args),
        out_specs=[vmem_spec()] * len(counts),
        scratch_shapes=[pltpu.VMEM((CAP, BLK, BLK), F32)],
        compiler_params=params(CODE_MIB),
        cost_estimate=pl.CostEstimate(
            flops=len(args) * CAP * BLK * BLK * 8, bytes_accessed=len(args) * CAP * BLK * BLK * 4,
            transcendentals=0),
    )(*args)


def sum_kernel(before, *refs):
    arrived, out = refs[:-1], refs[-1]
    scales = [scale_of(ref) for ref in arrived]
    for t in range(CAP):
        acc = before[t]
        for ref, scale in zip(arrived, scales):
            acc = acc + decode(ref, t, scale)
        out[t] = acc


def add_coded(before, arrived):
    count = len(arrived)
    return pl.pallas_call(
        sum_kernel,
        out_shape=jax.ShapeDtypeStruct((CAP, BLK, BLK), F32),
        in_specs=[vmem_spec()] * (1 + count),
        out_specs=vmem_spec(),
        compiler_params=params(10),
        cost_estimate=pl.CostEstimate(
            flops=count * CAP * BLK * BLK * 8, bytes_accessed=count * CAP * BLK * BLK * 2,
            transcendentals=0),
    )(before, *arrived)


def grad_kernel(ids, table, *refs):
    count = len(ids)
    blocks, mine, theirs, out, total = refs[:count], *refs[count:]
    side = table[SIDE_AT]
    core = table[SIDE_AT + 1]
    for k, place in enumerate(ids):
        dxh = COLS[place][1]
        first = pl.multiple_of((side if dxh == 0 else 1 - side) * 512, 512)
        for part, half in enumerate((core, 1 - core)):
            rows = pl.multiple_of(table[ROW_AT + half * 16 + place] * 256, 256)
            weights = (mine, theirs)[part][pl.ds(rows, 256), pl.ds(first, 512)]
            made = lax.dot_general(
                blocks[k][...], weights, (((1,), (1,)), ((), ())), preferred_element_type=F32)
            if k > 0:
                made = made + total[part]
            if k < count - 1:
                total[part] = made
            else:
                out[:, pl.ds(pl.multiple_of(half * 256, 256), 256)] = made.astype(out.dtype)


def grad_sum(table, ids, blocks, parts):
    count = len(ids)
    return pl.pallas_call(
        functools.partial(grad_kernel, tuple(ids)),
        out_shape=jax.ShapeDtypeStruct((512, 512), BF16),
        in_specs=[smem_spec()] + [vmem_spec()] * (count + 2),
        out_specs=vmem_spec(),
        scratch_shapes=[pltpu.VMEM((2, 512, 256), F32)],
        compiler_params=params(GRAD_MIB),
        cost_estimate=pl.CostEstimate(
            flops=2 * 512 ** 3 * count, bytes_accessed=(8 + count) * 1024 * 1024, transcendentals=0),
    )(table, *blocks, *parts)


def join_kernel(*refs):
    first = 0
    for part in refs[:-1]:
        refs[-1][first:first + part.shape[0], :] = part[...]
        first += part.shape[0]


def join(parts):
    rows = sum(part.shape[0] for part in parts)
    return pl.pallas_call(
        join_kernel,
        out_shape=jax.ShapeDtypeStruct((rows, parts[0].shape[1]), parts[0].dtype),
        in_specs=[vmem_spec()] * len(parts),
        out_specs=vmem_spec(),
        compiler_params=params(10),
        cost_estimate=pl.CostEstimate(
            flops=0, bytes_accessed=0, transcendentals=0),
    )(*parts)


def body(inputs, grad_out, weight, blocks, owner):
    row = lax.axis_index("row")
    col = lax.axis_index("col")
    core = lax.axis_index("srv")
    x_lo, y = row // 4, row % 4
    z, x_hi = col // 2, col % 2

    sign = 1 - 2 * core

    def ahead(v):
        return lax.ppermute(v, ("col", "srv"), z_shift(1))

    def back(v):
        return lax.ppermute(v, ("col", "srv"), z_shift(-1))

    def across(v):
        return lax.ppermute(v, "col", X_SWAP)

    def around(v):
        return lax.ppermute(v, ("row", "srv"), y_shift(1))

    def to_row(v, dx, dy):
        return lax.ppermute(v, "row", row_shift(dx, dy))

    def to_core(v):
        return lax.ppermute(v, "srv", CORE_SWAP)

    together = lax.optimization_barrier

    listed = blocks[0]
    owners = owner[0]
    live = listed[:, 0] >= 0
    order = jnp.arange(listed.shape[0], dtype=jnp.int32)
    same = owners[:, None] == owners[None, :]
    earlier = order[None, :] < order[:, None]
    rank = jnp.sum((same & earlier & live[None, :]).astype(jnp.int32), axis=1)
    position = jnp.where(live, owners * CAP + rank, -1)
    tile = jnp.where(live, listed[:, 1] * 4 + listed[:, 0] % 4, 0)
    fills = position[None, :] == order[:, None]
    slots = jnp.sum(jnp.where(fills, tile[None, :] + 1, 0), axis=1) - 1

    z_of = (z + sign * np.array([dz for dz, _ in COLS])) % 8
    col_of = z_of * 2 + (x_hi ^ np.array([dxh for _, dxh in COLS]))
    found = []
    for h in range(2):
        turn = np.array([t for t in range(4) for _ in range(2)])
        ids = (x_lo ^ np.array([dx for _ in range(4) for dx in range(2)])) * 4 + (y - (1 - 2 * h) * turn) % 4
        hit = ids[None, :] == z_of[:, None]
        found.append(jnp.sum(jnp.where(hit, np.arange(8)[None, :], 0), axis=1))
    dest = (x_lo ^ np.array([dx for dx, _ in DESTS])) * 4 + (y + np.array([dy for _, dy in DESTS])) % 4
    table = jnp.concatenate([
        v.astype(jnp.int32)
        for v in (col_of, *found, x_hi[None], core[None], dest * 2 + core, dest * 2 + 1 - core, slots)])
    xt = inputs.T

    half = lax.dynamic_slice_in_dim(weight, core * 256, 256, 0)
    far_half = to_row(half, 1, 0)
    r1, f1, own, table, xt = together((back(grad_out), ahead(grad_out), grad_out, table, xt))

    near_half, far_half, own, now = together((half, far_half, own, table))
    o0 = across(own)
    pair = join([near_half, far_half])
    w1 = around(pair)
    total = dense(None, now, xt, [grad_out, f1, r1], 0)
    o0, r2, f2, total = together((o0, back(r1), ahead(f1), total))

    w1, now = together((w1, table))
    w2 = around(w1)
    total = dense(total, now, xt, [f2, r2, o0], 3)
    of2, of1, r3, f3, total = together((across(f2), ahead(o0), back(r2), ahead(f2), total))

    w2, now = together((w2, table))
    w3 = around(w2)
    total = dense(total, now, xt, [f3, r3, of2], 6)
    or2, or1, f4, total = together((across(r2), back(o0), ahead(f3), total))

    w3, now = together((w3, table))
    mine = join([pair, w1, w2, w3])
    theirs = to_core(mine)
    total = dense(total, now, xt, [f4, of1, or1, or2], 9)
    of4, or3, of3, total = together((across(f4), back(or2), ahead(of2), total))

    total = dense(total, table, xt, [of3, or3, of4], LAST)
    cols = [grad_out, f1, r1, f2, r2, o0, f3, r3, of2, f4, of1, or1, or2, of3, or3, of4]

    theirs, early_table = together((theirs, table))
    other_early = to_core(pick(early_table, 0, EARLY, total))
    early = code(early_table, 0, EARLY, total, other_early, 0)
    *early, late_table = together((*early, table))
    other_late = to_core(pick(late_table, EARLY, 8, total))
    parts = [mine, theirs]
    late = code(late_table, EARLY, 8, total, other_late, 3)
    next_y, last_y, beside, opposite, own = late

    cross = to_row(early[0], 1, 0)
    ups, downs = to_row(early[1], 0, 1), to_row(early[2], 0, 3)
    near = [to_row(next_y, 0, 1), to_row(last_y, 0, 3)]
    beside, opposite = relay([(beside, [ups, downs]), (opposite, [cross])])
    pushed = add_coded(own, near)
    far = [to_row(beside, 1, 0), to_row(opposite, 0, 2)]
    pushed, grad_table = together((pushed, late_table))
    grad_in = grad_sum(grad_table, range(16), cols, parts)
    pushed, grad_in = together((pushed, grad_in))
    pushed = add_coded(pushed, far)
    return grad_in, pushed.reshape(1, CAP, BLK, BLK)


def solution(mesh):
    in_specs = (
        P(("row", "srv"), "col"),
        P(("row", "srv"), "col"),
        P("col", "row"),
        P("col", None, None),
        P("col", None),
    )
    out_specs = (P(("row", "srv"), "col"), P(("row", "srv"), "col", None, None))
    return jax.shard_map(body, mesh=mesh, in_specs=in_specs, out_specs=out_specs, check_vma=False)
```

```python
import functools

import jax
import jax.numpy as jnp
import numpy as np
from jax import lax
from jax.experimental import pallas as pl
from jax.experimental.pallas import tpu as pltpu
from jax.sharding import PartitionSpec as P

BLK = 128
CAP = 8
POWER = 9
TOP = 13.0
TAIL = 16
F32 = jnp.float32
BF16 = jnp.bfloat16

COLS = ((0, 0), (-1, 0), (1, 0), (-2, 0), (2, 0), (0, 1), (-3, 0), (3, 0), (-2, 1),
        (-4, 0), (-1, 1), (1, 1), (2, 1), (-3, 1), (3, 1), (-4, 1))
LAST = 13
DESTS = ((1, 2), (1, 1), (1, 3), (0, 1), (0, 3), (1, 0), (0, 2), (0, 0))
EARLY = 3
DENSE_MIB = PICK_MIB = CODE_MIB = GRAD_MIB = 10
PHASE_FLOPS = 30 * 10 ** 9
DENSE_MIB = PICK_MIB = CODE_MIB = GRAD_MIB = 10
COL_AT, ROW_AT, SIDE_AT, MINE_AT, THEIRS_AT, SLOT_AT = 0, 16, 48, 50, 58, 66


def z_shift(d):
    return [((z * 2 + h) * 2 + c, (((z + (1 - 2 * c) * d) % 8) * 2 + h) * 2 + c)
            for z in range(8) for h in range(2) for c in range(2)]


def y_shift(d):
    return [((l * 4 + y) * 2 + c, (l * 4 + (y + (1 - 2 * c) * d) % 4) * 2 + c)
            for l in range(2) for y in range(4) for c in range(2)]


def row_shift(dx, dy):
    return [(l * 4 + y, (l ^ dx) * 4 + (y + dy) % 4) for l in range(2) for y in range(4)]


X_SWAP = [(z * 2 + h, z * 2 + 1 - h) for z in range(8) for h in range(2)]
CORE_SWAP = [(0, 1), (1, 0)]


def hbm_spec():
    return pl.BlockSpec(memory_space=pltpu.HBM)


def smem_spec():
    return pl.BlockSpec(memory_space=pltpu.SMEM)


def vmem_spec():
    return pl.BlockSpec(memory_space=pltpu.VMEM)


def params(mib):
    return pltpu.CompilerParams(vmem_limit_bytes=mib * 1024 * 1024)


def dense_kernel(count, place, first, table, xt_ref, *refs):
    blocks = refs[:count]
    out = refs[count + (0 if first else 1)]
    for j in range(count):
        acc = jnp.dot(xt_ref[...], blocks[j][...], preferred_element_type=F32)
        at = table[COL_AT + place + j] * 16
        for cc in range(4):
            for rb in range(4):
                out[at + cc * 4 + rb] = acc[rb * BLK:(rb + 1) * BLK, cc * BLK:(cc + 1) * BLK]


def dense(total, table, xt, blocks, place):
    count = len(blocks)
    first = total is None
    args = [table, xt, *blocks] + ([] if first else [total])
    return pl.pallas_call(
        functools.partial(dense_kernel, count, place, first),
        out_shape=jax.ShapeDtypeStruct((256, BLK, BLK), F32),
        in_specs=[smem_spec(), vmem_spec()] + [vmem_spec()] * count + ([] if first else [vmem_spec()]),
        out_specs=vmem_spec(),
        input_output_aliases={} if first else {2 + count: 0},
        compiler_params=params(DENSE_MIB),
        cost_estimate=pl.CostEstimate(
            flops=PHASE_FLOPS, bytes_accessed=count * 3 * 512 * 1024, transcendentals=0),
    )(*args)


def slot_tile(table, owner_at, i):
    return table[SLOT_AT + table[owner_at + i // CAP] * CAP + i % CAP]


def pick_kernel(first, chunks, table, total, out):
    for i in range(chunks * CAP):
        out[i] = total[jnp.maximum(slot_tile(table, THEIRS_AT + first, i), 0)]


def pick(table, first, last, total):
    chunks = last - first
    return pl.pallas_call(
        functools.partial(pick_kernel, first, chunks),
        out_shape=jax.ShapeDtypeStruct((chunks * CAP, BLK, BLK), F32),
        in_specs=[smem_spec(), vmem_spec()],
        out_specs=vmem_spec(),
        compiler_params=params(PICK_MIB),
        cost_estimate=pl.CostEstimate(
            flops=0, bytes_accessed=chunks * CAP * BLK * BLK * 8, transcendentals=0),
    )(table, total)


def encode(held, most, out):
    level = jnp.ceil(jnp.log2(jnp.maximum(most, 1e-30)))
    scale = jnp.exp2(TOP - level)
    for t in range(CAP):
        v = held[t] * scale
        v2 = v * v
        v4 = v2 * v2
        out[t * BLK:(t + 1) * BLK, :] = (v4 * v4 * v).astype(BF16)
    out[CAP * BLK:, :] = jnp.broadcast_to(level, (TAIL, BLK)).astype(BF16)


def scale_of(ref):
    return ref[CAP * BLK:CAP * BLK + TAIL, :].astype(F32)[0:1, :] - TOP


def decode(ref, t, scale):
    y = ref[t * BLK:(t + 1) * BLK, :].astype(F32)
    size = jnp.exp2(jnp.log2(jnp.maximum(jnp.abs(y), 1e-37)) * (1.0 / POWER) + scale)
    size = jnp.where(jnp.abs(y) > 1e-37, size, 0.0)
    return jnp.where(y < 0, -size, size)


def largest(most, tile):
    return jnp.maximum(most, jnp.max(jnp.abs(tile), axis=0, keepdims=True))


def code_kernel(at, coded, plain, table, total, other, *refs):
    chunks = coded + plain
    outs, held = refs[:chunks], refs[chunks]
    for m in range(chunks):
        most = jnp.zeros((1, BLK), F32)
        for t in range(CAP):
            i = m * CAP + t
            tile = slot_tile(table, MINE_AT + at, i)
            both = jnp.where(tile >= 0, total[jnp.maximum(tile, 0)] + other[i], 0.0)
            if m >= coded:
                outs[m][t] = both
            else:
                held[t] = both
                most = largest(most, both)
        if m < coded:
            encode(held, most, outs[m])


def code(table, first, last, total, other, plain):
    chunks = last - first
    coded = chunks - plain
    return pl.pallas_call(
        functools.partial(code_kernel, first, coded, plain),
        out_shape=[jax.ShapeDtypeStruct((CAP * BLK + TAIL, BLK), BF16)] * coded
        + [jax.ShapeDtypeStruct((CAP, BLK, BLK), F32)] * plain,
        in_specs=[smem_spec(), vmem_spec(), vmem_spec()],
        out_specs=[vmem_spec()] * chunks,
        scratch_shapes=[pltpu.VMEM((CAP, BLK, BLK), F32)],
        compiler_params=params(CODE_MIB),
        cost_estimate=pl.CostEstimate(
            flops=chunks * CAP * BLK * BLK * 8, bytes_accessed=chunks * CAP * BLK * BLK * 10,
            transcendentals=0),
    )(table, total, other)


def relay_kernel(counts, *refs):
    outs, held = refs[-1 - len(counts):-1], refs[-1]
    at = 0
    for m, count in enumerate(counts):
        before, arrived = refs[at], refs[at + 1:at + 1 + count]
        at += 1 + count
        scales = [scale_of(ref) for ref in arrived]
        most = jnp.zeros((1, BLK), F32)
        for t in range(CAP):
            acc = before[t]
            for ref, scale in zip(arrived, scales):
                acc = acc + decode(ref, t, scale)
            held[t] = acc
            most = largest(most, acc)
        encode(held, most, outs[m])


def relay(groups):
    counts = tuple(len(arrived) for _, arrived in groups)
    args = [v for before, arrived in groups for v in (before, *arrived)]
    return pl.pallas_call(
        functools.partial(relay_kernel, counts),
        out_shape=[jax.ShapeDtypeStruct((CAP * BLK + TAIL, BLK), BF16)] * len(counts),
        in_specs=[vmem_spec()] * len(args),
        out_specs=[vmem_spec()] * len(counts),
        scratch_shapes=[pltpu.VMEM((CAP, BLK, BLK), F32)],
        compiler_params=params(CODE_MIB),
        cost_estimate=pl.CostEstimate(
            flops=len(args) * CAP * BLK * BLK * 8, bytes_accessed=len(args) * CAP * BLK * BLK * 4,
            transcendentals=0),
    )(*args)


def sum_kernel(before, *refs):
    arrived, out = refs[:-1], refs[-1]
    scales = [scale_of(ref) for ref in arrived]
    for t in range(CAP):
        acc = before[t]
        for ref, scale in zip(arrived, scales):
            acc = acc + decode(ref, t, scale)
        out[t] = acc


def add_coded(before, arrived):
    count = len(arrived)
    return pl.pallas_call(
        sum_kernel,
        out_shape=jax.ShapeDtypeStruct((CAP, BLK, BLK), F32),
        in_specs=[vmem_spec()] * (1 + count),
        out_specs=vmem_spec(),
        compiler_params=params(10),
        cost_estimate=pl.CostEstimate(
            flops=count * CAP * BLK * BLK * 8, bytes_accessed=count * CAP * BLK * BLK * 2,
            transcendentals=0),
    )(before, *arrived)


def grad_kernel(ids, last, table, *refs):
    count = len(ids)
    blocks, mine, theirs = refs[:count], refs[count], refs[count + 1]
    before, out, total = refs[count + 2] if last else None, refs[-2], refs[-1]
    side = table[SIDE_AT]
    core = table[SIDE_AT + 1]
    for k, place in enumerate(ids):
        dxh = COLS[place][1]
        first = pl.multiple_of((side if dxh == 0 else 1 - side) * 512, 512)
        for part, half in enumerate((core, 1 - core)):
            rows = pl.multiple_of(table[ROW_AT + half * 16 + place] * 256, 256)
            weights = (mine, theirs)[part][pl.ds(rows, 256), pl.ds(first, 512)]
            made = lax.dot_general(
                blocks[k][...], weights, (((1,), (1,)), ((), ())), preferred_element_type=F32)
            if k > 0:
                made = made + total[part]
            elif last:
                made = made + before[part]
            if k < count - 1:
                total[part] = made
            elif last:
                out[:, pl.ds(pl.multiple_of(half * 256, 256), 256)] = made.astype(out.dtype)
            else:
                out[part] = made


def grad_sum(table, ids, blocks, parts, before=None):
    count = len(ids)
    last = before is not None
    return pl.pallas_call(
        functools.partial(grad_kernel, tuple(ids), last),
        out_shape=jax.ShapeDtypeStruct((512, 512), BF16) if last
        else jax.ShapeDtypeStruct((2, 512, 256), F32),
        in_specs=[smem_spec()] + [vmem_spec()] * (count + 2 + last),
        out_specs=vmem_spec(),
        scratch_shapes=[pltpu.VMEM((2, 512, 256), F32)],
        compiler_params=params(GRAD_MIB),
        cost_estimate=pl.CostEstimate(flops=0, bytes_accessed=0, transcendentals=0),
    )(table, *blocks, *parts, *([before] if last else []))


def join_kernel(*refs):
    first = 0
    for part in refs[:-1]:
        refs[-1][first:first + part.shape[0], :] = part[...]
        first += part.shape[0]


def join(parts):
    rows = sum(part.shape[0] for part in parts)
    return pl.pallas_call(
        join_kernel,
        out_shape=jax.ShapeDtypeStruct((rows, parts[0].shape[1]), parts[0].dtype),
        in_specs=[vmem_spec()] * len(parts),
        out_specs=vmem_spec(),
        compiler_params=params(10),
        cost_estimate=pl.CostEstimate(
            flops=0, bytes_accessed=0, transcendentals=0),
    )(*parts)


def body(inputs, grad_out, weight, blocks, owner):
    row = lax.axis_index("row")
    col = lax.axis_index("col")
    core = lax.axis_index("srv")
    x_lo, y = row // 4, row % 4
    z, x_hi = col // 2, col % 2

    sign = 1 - 2 * core

    def ahead(v):
        return lax.ppermute(v, ("col", "srv"), z_shift(1))

    def back(v):
        return lax.ppermute(v, ("col", "srv"), z_shift(-1))

    def across(v):
        return lax.ppermute(v, "col", X_SWAP)

    def around(v):
        return lax.ppermute(v, ("row", "srv"), y_shift(1))

    def to_row(v, dx, dy):
        return lax.ppermute(v, "row", row_shift(dx, dy))

    def to_core(v):
        return lax.ppermute(v, "srv", CORE_SWAP)

    together = lax.optimization_barrier

    listed = blocks[0]
    owners = owner[0]
    live = listed[:, 0] >= 0
    order = jnp.arange(listed.shape[0], dtype=jnp.int32)
    same = owners[:, None] == owners[None, :]
    earlier = order[None, :] < order[:, None]
    rank = jnp.sum((same & earlier & live[None, :]).astype(jnp.int32), axis=1)
    position = jnp.where(live, owners * CAP + rank, -1)
    tile = jnp.where(live, listed[:, 1] * 4 + listed[:, 0] % 4, 0)
    fills = position[None, :] == order[:, None]
    slots = jnp.sum(jnp.where(fills, tile[None, :] + 1, 0), axis=1) - 1

    z_of = (z + sign * np.array([dz for dz, _ in COLS])) % 8
    col_of = z_of * 2 + (x_hi ^ np.array([dxh for _, dxh in COLS]))
    found = []
    for h in range(2):
        turn = np.array([t for t in range(4) for _ in range(2)])
        ids = (x_lo ^ np.array([dx for _ in range(4) for dx in range(2)])) * 4 + (y - (1 - 2 * h) * turn) % 4
        hit = ids[None, :] == z_of[:, None]
        found.append(jnp.sum(jnp.where(hit, np.arange(8)[None, :], 0), axis=1))
    dest = (x_lo ^ np.array([dx for dx, _ in DESTS])) * 4 + (y + np.array([dy for _, dy in DESTS])) % 4
    table = jnp.concatenate([
        v.astype(jnp.int32)
        for v in (col_of, *found, x_hi[None], core[None], dest * 2 + core, dest * 2 + 1 - core, slots)])
    xt = inputs.T

    half = lax.dynamic_slice_in_dim(weight, core * 256, 256, 0)
    far_half = to_row(half, 1, 0)
    r1, f1, own, table, xt = together((back(grad_out), ahead(grad_out), grad_out, table, xt))

    near_half, far_half, own, now = together((half, far_half, own, table))
    o0 = across(own)
    pair = join([near_half, far_half])
    w1 = around(pair)
    total = dense(None, now, xt, [grad_out, f1, r1], 0)
    o0, r2, f2, total = together((o0, back(r1), ahead(f1), total))

    w1, now = together((w1, table))
    w2 = around(w1)
    total = dense(total, now, xt, [f2, r2, o0], 3)
    of2, of1, r3, f3, total = together((across(f2), ahead(o0), back(r2), ahead(f2), total))

    w2, now = together((w2, table))
    w3 = around(w2)
    total = dense(total, now, xt, [f3, r3, of2], 6)
    or2, or1, f4, total = together((across(r2), back(o0), ahead(f3), total))

    w3, now = together((w3, table))
    mine = join([pair, w1, w2, w3])
    theirs = to_core(mine)
    total = dense(total, now, xt, [f4, of1, or1, or2], 9)
    of4, or3, of3, total = together((across(f4), back(or2), ahead(of2), total))

    total = dense(total, table, xt, [of3, or3, of4], LAST)
    cols = [grad_out, f1, r1, f2, r2, o0, f3, r3, of2, f4, of1, or1, or2, of3, or3, of4]

    theirs, early_table = together((theirs, table))
    parts = [mine, theirs]
    other_early = to_core(pick(early_table, 0, EARLY, total))
    first_half = grad_sum(early_table, range(8), cols[:8], parts)
    first_half, early_table = together((first_half, early_table))
    early = code(early_table, 0, EARLY, total, other_early, 0)
    *early, late_table = together((*early, table))
    other_late = to_core(pick(late_table, EARLY, 8, total))
    late = code(late_table, EARLY, 8, total, other_late, 3)
    next_y, last_y, beside, opposite, own = late

    cross = to_row(early[0], 1, 0)
    ups, downs = to_row(early[1], 0, 1), to_row(early[2], 0, 3)
    near = [to_row(next_y, 0, 1), to_row(last_y, 0, 3)]
    beside, opposite = relay([(beside, [ups, downs]), (opposite, [cross])])
    beside, opposite, grad_table = together((beside, opposite, late_table))
    far = [to_row(beside, 1, 0), to_row(opposite, 0, 2)]
    grad_in = grad_sum(grad_table, range(8, 16), cols[8:], parts, first_half)
    own, grad_in = together((own, grad_in))
    pushed = add_coded(own, near)
    pushed = add_coded(pushed, far)
    return grad_in, pushed.reshape(1, CAP, BLK, BLK)


def solution(mesh):
    in_specs = (
        P(("row", "srv"), "col"),
        P(("row", "srv"), "col"),
        P("col", "row"),
        P("col", None, None),
        P("col", None),
    )
    out_specs = (P(("row", "srv"), "col"), P(("row", "srv"), "col", None, None))
    return jax.shard_map(body, mesh=mesh, in_specs=in_specs, out_specs=out_specs, check_vma=False)
```

```python
import functools

import jax
import jax.numpy as jnp
import numpy as np
from jax import lax
from jax.experimental import pallas as pl
from jax.experimental.pallas import tpu as pltpu
from jax.sharding import PartitionSpec as P

BLK = 128
CAP = 8
POWER = 9
TOP = 13.0
TAIL = 16
F32 = jnp.float32
BF16 = jnp.bfloat16

COLS = ((0, 0), (-1, 0), (1, 0), (-2, 0), (2, 0), (0, 1), (-3, 0), (3, 0), (-2, 1),
        (-4, 0), (-1, 1), (1, 1), (2, 1), (-3, 1), (3, 1), (-4, 1))
LAST = 13
DESTS = ((1, 2), (1, 1), (1, 3), (0, 1), (0, 3), (1, 0), (0, 2), (0, 0))
EARLY = 3
DENSE_MIB = PICK_MIB = CODE_MIB = GRAD_MIB = 10
PHASE_FLOPS = 30 * 10 ** 9
DENSE_MIB = PICK_MIB = CODE_MIB = GRAD_MIB = 10
COL_AT, ROW_AT, SIDE_AT, MINE_AT, THEIRS_AT, SLOT_AT = 0, 16, 48, 50, 58, 66


def z_shift(d):
    return [((z * 2 + h) * 2 + c, (((z + (1 - 2 * c) * d) % 8) * 2 + h) * 2 + c)
            for z in range(8) for h in range(2) for c in range(2)]


def y_shift(d):
    return [((l * 4 + y) * 2 + c, (l * 4 + (y + (1 - 2 * c) * d) % 4) * 2 + c)
            for l in range(2) for y in range(4) for c in range(2)]


def row_shift(dx, dy):
    return [(l * 4 + y, (l ^ dx) * 4 + (y + dy) % 4) for l in range(2) for y in range(4)]


X_SWAP = [(z * 2 + h, z * 2 + 1 - h) for z in range(8) for h in range(2)]
CORE_SWAP = [(0, 1), (1, 0)]


def hbm_spec():
    return pl.BlockSpec(memory_space=pltpu.HBM)


def smem_spec():
    return pl.BlockSpec(memory_space=pltpu.SMEM)


def vmem_spec():
    return pl.BlockSpec(memory_space=pltpu.VMEM)


def params(mib):
    return pltpu.CompilerParams(vmem_limit_bytes=mib * 1024 * 1024)


def dense_kernel(count, place, first, table, xt_ref, *refs):
    blocks = refs[:count]
    out = refs[count + (0 if first else 1)]
    for j in range(count):
        acc = jnp.dot(xt_ref[...], blocks[j][...], preferred_element_type=F32)
        at = table[COL_AT + place + j] * 16
        for cc in range(4):
            for rb in range(4):
                out[at + cc * 4 + rb] = acc[rb * BLK:(rb + 1) * BLK, cc * BLK:(cc + 1) * BLK]


def dense(total, table, xt, blocks, place):
    count = len(blocks)
    first = total is None
    args = [table, xt, *blocks] + ([] if first else [total])
    return pl.pallas_call(
        functools.partial(dense_kernel, count, place, first),
        out_shape=jax.ShapeDtypeStruct((256, BLK, BLK), F32),
        in_specs=[smem_spec(), vmem_spec()] + [vmem_spec()] * count + ([] if first else [vmem_spec()]),
        out_specs=vmem_spec(),
        input_output_aliases={} if first else {2 + count: 0},
        compiler_params=params(DENSE_MIB),
        cost_estimate=pl.CostEstimate(
            flops=PHASE_FLOPS, bytes_accessed=count * 3 * 512 * 1024, transcendentals=0),
    )(*args)


def slot_tile(table, owner_at, i):
    return table[SLOT_AT + table[owner_at + i // CAP] * CAP + i % CAP]


def pick_kernel(first, chunks, table, total, out):
    for i in range(chunks * CAP):
        out[i] = total[jnp.maximum(slot_tile(table, THEIRS_AT + first, i), 0)]


def pick(table, first, last, total):
    chunks = last - first
    return pl.pallas_call(
        functools.partial(pick_kernel, first, chunks),
        out_shape=jax.ShapeDtypeStruct((chunks * CAP, BLK, BLK), F32),
        in_specs=[smem_spec(), vmem_spec()],
        out_specs=vmem_spec(),
        compiler_params=params(PICK_MIB),
        cost_estimate=pl.CostEstimate(
            flops=0, bytes_accessed=chunks * CAP * BLK * BLK * 8, transcendentals=0),
    )(table, total)


def encode(held, most, out):
    level = jnp.ceil(jnp.log2(jnp.maximum(most, 1e-30)))
    scale = jnp.exp2(TOP - level)
    for t in range(CAP):
        v = held[t] * scale
        v2 = v * v
        v4 = v2 * v2
        out[t * BLK:(t + 1) * BLK, :] = (v4 * v4 * v).astype(BF16)
    out[CAP * BLK:, :] = jnp.broadcast_to(level, (TAIL, BLK)).astype(BF16)


def scale_of(ref):
    return ref[CAP * BLK:CAP * BLK + TAIL, :].astype(F32)[0:1, :] - TOP


def decode(ref, t, scale):
    y = ref[t * BLK:(t + 1) * BLK, :].astype(F32)
    size = jnp.exp2(jnp.log2(jnp.maximum(jnp.abs(y), 1e-37)) * (1.0 / POWER) + scale)
    size = jnp.where(jnp.abs(y) > 1e-37, size, 0.0)
    return jnp.where(y < 0, -size, size)


def largest(most, tile):
    return jnp.maximum(most, jnp.max(jnp.abs(tile), axis=0, keepdims=True))


def code_kernel(at, coded, plain, table, total, other, *refs):
    chunks = coded + plain
    outs, held = refs[:chunks], refs[chunks]
    for m in range(chunks):
        most = jnp.zeros((1, BLK), F32)
        for t in range(CAP):
            i = m * CAP + t
            tile = slot_tile(table, MINE_AT + at, i)
            both = jnp.where(tile >= 0, total[jnp.maximum(tile, 0)] + other[i], 0.0)
            if m >= coded:
                outs[m][t] = both
            else:
                held[t] = both
                most = largest(most, both)
        if m < coded:
            encode(held, most, outs[m])


def code(table, first, last, total, other, plain):
    chunks = last - first
    coded = chunks - plain
    return pl.pallas_call(
        functools.partial(code_kernel, first, coded, plain),
        out_shape=[jax.ShapeDtypeStruct((CAP * BLK + TAIL, BLK), BF16)] * coded
        + [jax.ShapeDtypeStruct((CAP, BLK, BLK), F32)] * plain,
        in_specs=[smem_spec(), vmem_spec(), vmem_spec()],
        out_specs=[vmem_spec()] * chunks,
        scratch_shapes=[pltpu.VMEM((CAP, BLK, BLK), F32)],
        compiler_params=params(CODE_MIB),
        cost_estimate=pl.CostEstimate(
            flops=chunks * CAP * BLK * BLK * 8, bytes_accessed=chunks * CAP * BLK * BLK * 10,
            transcendentals=0),
    )(table, total, other)


def relay_kernel(counts, *refs):
    outs, held = refs[-1 - len(counts):-1], refs[-1]
    at = 0
    for m, count in enumerate(counts):
        before, arrived = refs[at], refs[at + 1:at + 1 + count]
        at += 1 + count
        scales = [scale_of(ref) for ref in arrived]
        most = jnp.zeros((1, BLK), F32)
        for t in range(CAP):
            acc = before[t]
            for ref, scale in zip(arrived, scales):
                acc = acc + decode(ref, t, scale)
            held[t] = acc
            most = largest(most, acc)
        encode(held, most, outs[m])


def relay(groups):
    counts = tuple(len(arrived) for _, arrived in groups)
    args = [v for before, arrived in groups for v in (before, *arrived)]
    return pl.pallas_call(
        functools.partial(relay_kernel, counts),
        out_shape=[jax.ShapeDtypeStruct((CAP * BLK + TAIL, BLK), BF16)] * len(counts),
        in_specs=[vmem_spec()] * len(args),
        out_specs=[vmem_spec()] * len(counts),
        scratch_shapes=[pltpu.VMEM((CAP, BLK, BLK), F32)],
        compiler_params=params(CODE_MIB),
        cost_estimate=pl.CostEstimate(
            flops=len(args) * CAP * BLK * BLK * 8, bytes_accessed=len(args) * CAP * BLK * BLK * 4,
            transcendentals=0),
    )(*args)


def sum_kernel(before, *refs):
    arrived, out = refs[:-1], refs[-1]
    scales = [scale_of(ref) for ref in arrived]
    for t in range(CAP):
        acc = before[t]
        for ref, scale in zip(arrived, scales):
            acc = acc + decode(ref, t, scale)
        out[t] = acc


def add_coded(before, arrived):
    count = len(arrived)
    return pl.pallas_call(
        sum_kernel,
        out_shape=jax.ShapeDtypeStruct((CAP, BLK, BLK), F32),
        in_specs=[vmem_spec()] * (1 + count),
        out_specs=vmem_spec(),
        compiler_params=params(10),
        cost_estimate=pl.CostEstimate(
            flops=count * CAP * BLK * BLK * 8, bytes_accessed=count * CAP * BLK * BLK * 2,
            transcendentals=0),
    )(before, *arrived)


def grad_kernel(ids, last, table, *refs):
    count = len(ids)
    blocks, mine, theirs = refs[:count], refs[count], refs[count + 1]
    before, out, total = refs[count + 2] if last else None, refs[-2], refs[-1]
    side = table[SIDE_AT]
    core = table[SIDE_AT + 1]
    for k, place in enumerate(ids):
        dxh = COLS[place][1]
        first = pl.multiple_of((side if dxh == 0 else 1 - side) * 512, 512)
        for part, half in enumerate((core, 1 - core)):
            rows = pl.multiple_of(table[ROW_AT + half * 16 + place] * 256, 256)
            weights = (mine, theirs)[part][pl.ds(rows, 256), pl.ds(first, 512)]
            made = lax.dot_general(
                blocks[k][...], weights, (((1,), (1,)), ((), ())), preferred_element_type=F32)
            if k > 0:
                made = made + total[part]
            elif last:
                made = made + before[part]
            if k < count - 1:
                total[part] = made
            elif last:
                out[:, pl.ds(pl.multiple_of(half * 256, 256), 256)] = made.astype(out.dtype)
            else:
                out[part] = made


def grad_sum(table, ids, blocks, parts, before=None):
    count = len(ids)
    last = before is not None
    return pl.pallas_call(
        functools.partial(grad_kernel, tuple(ids), last),
        out_shape=jax.ShapeDtypeStruct((512, 512), BF16) if last
        else jax.ShapeDtypeStruct((2, 512, 256), F32),
        in_specs=[smem_spec()] + [vmem_spec()] * (count + 2 + last),
        out_specs=vmem_spec(),
        scratch_shapes=[pltpu.VMEM((2, 512, 256), F32)],
        compiler_params=params(GRAD_MIB),
        cost_estimate=pl.CostEstimate(flops=0, bytes_accessed=0, transcendentals=0),
    )(table, *blocks, *parts, *([before] if last else []))


def join_kernel(*refs):
    first = 0
    for part in refs[:-1]:
        refs[-1][first:first + part.shape[0], :] = part[...]
        first += part.shape[0]


def join(parts):
    rows = sum(part.shape[0] for part in parts)
    return pl.pallas_call(
        join_kernel,
        out_shape=jax.ShapeDtypeStruct((rows, parts[0].shape[1]), parts[0].dtype),
        in_specs=[vmem_spec()] * len(parts),
        out_specs=vmem_spec(),
        compiler_params=params(10),
        cost_estimate=pl.CostEstimate(
            flops=0, bytes_accessed=0, transcendentals=0),
    )(*parts)


def body(inputs, grad_out, weight, blocks, owner):
    row = lax.axis_index("row")
    col = lax.axis_index("col")
    core = lax.axis_index("srv")
    x_lo, y = row // 4, row % 4
    z, x_hi = col // 2, col % 2

    sign = 1 - 2 * core

    def ahead(v):
        return lax.ppermute(v, ("col", "srv"), z_shift(1))

    def back(v):
        return lax.ppermute(v, ("col", "srv"), z_shift(-1))

    def across(v):
        return lax.ppermute(v, "col", X_SWAP)

    def around(v):
        return lax.ppermute(v, ("row", "srv"), y_shift(1))

    def to_row(v, dx, dy):
        return lax.ppermute(v, "row", row_shift(dx, dy))

    def to_core(v):
        return lax.ppermute(v, "srv", CORE_SWAP)

    together = lax.optimization_barrier

    listed = blocks[0]
    owners = owner[0]
    live = listed[:, 0] >= 0
    order = jnp.arange(listed.shape[0], dtype=jnp.int32)
    same = owners[:, None] == owners[None, :]
    earlier = order[None, :] < order[:, None]
    rank = jnp.sum((same & earlier & live[None, :]).astype(jnp.int32), axis=1)
    position = jnp.where(live, owners * CAP + rank, -1)
    tile = jnp.where(live, listed[:, 1] * 4 + listed[:, 0] % 4, 0)
    fills = position[None, :] == order[:, None]
    slots = jnp.sum(jnp.where(fills, tile[None, :] + 1, 0), axis=1) - 1

    z_of = (z + sign * np.array([dz for dz, _ in COLS])) % 8
    col_of = z_of * 2 + (x_hi ^ np.array([dxh for _, dxh in COLS]))
    found = []
    for h in range(2):
        turn = np.array([t for t in range(4) for _ in range(2)])
        ids = (x_lo ^ np.array([dx for _ in range(4) for dx in range(2)])) * 4 + (y - (1 - 2 * h) * turn) % 4
        hit = ids[None, :] == z_of[:, None]
        found.append(jnp.sum(jnp.where(hit, np.arange(8)[None, :], 0), axis=1))
    dest = (x_lo ^ np.array([dx for dx, _ in DESTS])) * 4 + (y + np.array([dy for _, dy in DESTS])) % 4
    table = jnp.concatenate([
        v.astype(jnp.int32)
        for v in (col_of, *found, x_hi[None], core[None], dest * 2 + core, dest * 2 + 1 - core, slots)])
    xt = inputs.T

    half = lax.dynamic_slice_in_dim(weight, core * 256, 256, 0)
    far_half = to_row(half, 1, 0)
    r1, f1, own, table, xt = together((back(grad_out), ahead(grad_out), grad_out, table, xt))

    near_half, far_half, own, now = together((half, far_half, own, table))
    f2, r2 = ahead(f1), back(r1)
    o0 = across(own)
    pair = join([near_half, far_half])
    w1 = around(pair)
    total = dense(None, now, xt, [grad_out, f1, r1], 0)
    r2, f2, total = together((r2, f2, total))

    w1, now = together((w1, table))
    w2 = around(w1)
    total = dense(total, now, xt, [f2, r2, o0], 3)
    f3, r3, of1 = ahead(f2), back(r2), ahead(o0)
    of2, of1, r3, f3, total = together((across(f2), of1, r3, f3, total))

    w2, now = together((w2, table))
    w3 = around(w2)
    total = dense(total, now, xt, [f3, r3, of2], 6)
    or2, or1, f4, total = together((across(r2), back(o0), ahead(f3), total))

    w3, now = together((w3, table))
    mine = join([pair, w1, w2, w3])
    theirs = to_core(mine)
    total = dense(total, now, xt, [f4, of1, or1, or2], 9)
    of3, or3 = ahead(of2), back(or2)
    of4, or3, of3, total = together((across(f4), or3, of3, total))

    total = dense(total, table, xt, [of3, or3, of4], LAST)
    cols = [grad_out, f1, r1, f2, r2, o0, f3, r3, of2, f4, of1, or1, or2, of3, or3, of4]

    theirs, early_table = together((theirs, table))
    parts = [mine, theirs]
    other_early = to_core(pick(early_table, 0, EARLY, total))
    first_half = grad_sum(early_table, range(8), cols[:8], parts)
    first_half, early_table = together((first_half, early_table))
    early = code(early_table, 0, EARLY, total, other_early, 0)
    *early, late_table = together((*early, table))
    other_late = to_core(pick(late_table, EARLY, 8, total))
    late = code(late_table, EARLY, 8, total, other_late, 3)
    next_y, last_y, beside, opposite, own = late

    cross = to_row(early[0], 1, 0)
    ups, downs = to_row(early[1], 0, 1), to_row(early[2], 0, 3)
    near = [to_row(next_y, 0, 1), to_row(last_y, 0, 3)]
    beside, opposite = relay([(beside, [ups, downs]), (opposite, [cross])])
    beside, opposite, grad_table = together((beside, opposite, late_table))
    far = [to_row(beside, 1, 0), to_row(opposite, 0, 2)]
    grad_in = grad_sum(grad_table, range(8, 16), cols[8:], parts, first_half)
    own, grad_in = together((own, grad_in))
    pushed = add_coded(own, near)
    pushed = add_coded(pushed, far)
    return grad_in, pushed.reshape(1, CAP, BLK, BLK)


def solution(mesh):
    in_specs = (
        P(("row", "srv"), "col"),
        P(("row", "srv"), "col"),
        P("col", "row"),
        P("col", None, None),
        P("col", None),
    )
    out_specs = (P(("row", "srv"), "col"), P(("row", "srv"), "col", None, None))
    return jax.shard_map(body, mesh=mesh, in_specs=in_specs, out_specs=out_specs, check_vma=False)
```

```python
import functools

import jax
import jax.numpy as jnp
import numpy as np
from jax import lax
from jax.experimental import pallas as pl
from jax.experimental.pallas import tpu as pltpu
from jax.sharding import PartitionSpec as P

BLK = 128
CAP = 8
POWER = 9
TOP = 13.0
TAIL = 16
F32 = jnp.float32
BF16 = jnp.bfloat16

COLS = ((0, 0), (-1, 0), (1, 0), (-2, 0), (2, 0), (0, 1), (-3, 0), (3, 0), (-2, 1),
        (-4, 0), (-1, 1), (1, 1), (2, 1), (-3, 1), (3, 1), (-4, 1))
LAST = 13
DESTS = ((1, 2), (1, 1), (1, 3), (0, 1), (0, 3), (1, 0), (0, 2), (0, 0))
EARLY = 3
DENSE_MIB = PICK_MIB = CODE_MIB = GRAD_MIB = 10
PHASE_FLOPS = 30 * 10 ** 9
DENSE_MIB = PICK_MIB = CODE_MIB = GRAD_MIB = 10
COL_AT, ROW_AT, SIDE_AT, MINE_AT, THEIRS_AT, SLOT_AT = 0, 16, 48, 50, 58, 66


def z_shift(d):
    return [((z * 2 + h) * 2 + c, (((z + (1 - 2 * c) * d) % 8) * 2 + h) * 2 + c)
            for z in range(8) for h in range(2) for c in range(2)]


def y_shift(d):
    return [((l * 4 + y) * 2 + c, (l * 4 + (y + (1 - 2 * c) * d) % 4) * 2 + c)
            for l in range(2) for y in range(4) for c in range(2)]


def row_shift(dx, dy):
    return [(l * 4 + y, (l ^ dx) * 4 + (y + dy) % 4) for l in range(2) for y in range(4)]


X_SWAP = [(z * 2 + h, z * 2 + 1 - h) for z in range(8) for h in range(2)]
CORE_SWAP = [(0, 1), (1, 0)]


def hbm_spec():
    return pl.BlockSpec(memory_space=pltpu.HBM)


def smem_spec():
    return pl.BlockSpec(memory_space=pltpu.SMEM)


def vmem_spec():
    return pl.BlockSpec(memory_space=pltpu.VMEM)


def params(mib):
    return pltpu.CompilerParams(vmem_limit_bytes=mib * 1024 * 1024)


def dense_kernel(count, place, first, table, xt_ref, *refs):
    blocks = refs[:count]
    out = refs[count + (0 if first else 1)]
    for j in range(count):
        acc = jnp.dot(xt_ref[...], blocks[j][...], preferred_element_type=F32)
        at = table[COL_AT + place + j] * 16
        for cc in range(4):
            for rb in range(4):
                out[at + cc * 4 + rb] = acc[rb * BLK:(rb + 1) * BLK, cc * BLK:(cc + 1) * BLK]


def dense(total, table, xt, blocks, place):
    count = len(blocks)
    first = total is None
    args = [table, xt, *blocks] + ([] if first else [total])
    return pl.pallas_call(
        functools.partial(dense_kernel, count, place, first),
        out_shape=jax.ShapeDtypeStruct((256, BLK, BLK), F32),
        in_specs=[smem_spec(), vmem_spec()] + [vmem_spec()] * count + ([] if first else [vmem_spec()]),
        out_specs=vmem_spec(),
        input_output_aliases={} if first else {2 + count: 0},
        compiler_params=params(DENSE_MIB),
        cost_estimate=pl.CostEstimate(
            flops=PHASE_FLOPS, bytes_accessed=count * 3 * 512 * 1024, transcendentals=0),
    )(*args)


def slot_tile(table, owner_at, i):
    return table[SLOT_AT + table[owner_at + i // CAP] * CAP + i % CAP]


def pick_kernel(first, chunks, table, total, out):
    for i in range(chunks * CAP):
        out[i] = total[jnp.maximum(slot_tile(table, THEIRS_AT + first, i), 0)]


def pick(table, first, last, total):
    chunks = last - first
    return pl.pallas_call(
        functools.partial(pick_kernel, first, chunks),
        out_shape=jax.ShapeDtypeStruct((chunks * CAP, BLK, BLK), F32),
        in_specs=[smem_spec(), vmem_spec()],
        out_specs=vmem_spec(),
        compiler_params=params(PICK_MIB),
        cost_estimate=pl.CostEstimate(
            flops=0, bytes_accessed=chunks * CAP * BLK * BLK * 8, transcendentals=0),
    )(table, total)


def encode(held, most, out):
    level = jnp.ceil(jnp.log2(jnp.maximum(most, 1e-30)))
    scale = jnp.exp2(TOP - level)
    for t in range(CAP):
        v = held[t] * scale
        v2 = v * v
        v4 = v2 * v2
        out[t * BLK:(t + 1) * BLK, :] = (v4 * v4 * v).astype(BF16)
    out[CAP * BLK:, :] = jnp.broadcast_to(level, (TAIL, BLK)).astype(BF16)


def scale_of(ref):
    return ref[CAP * BLK:CAP * BLK + TAIL, :].astype(F32)[0:1, :] - TOP


def decode(ref, t, scale):
    y = ref[t * BLK:(t + 1) * BLK, :].astype(F32)
    size = jnp.exp2(jnp.log2(jnp.maximum(jnp.abs(y), 1e-37)) * (1.0 / POWER) + scale)
    size = jnp.where(jnp.abs(y) > 1e-37, size, 0.0)
    return jnp.where(y < 0, -size, size)


def largest(most, tile):
    return jnp.maximum(most, jnp.max(jnp.abs(tile), axis=0, keepdims=True))


def code_kernel(at, coded, plain, table, total, other, *refs):
    chunks = coded + plain
    outs, held = refs[:chunks], refs[chunks]
    for m in range(chunks):
        most = jnp.zeros((1, BLK), F32)
        for t in range(CAP):
            i = m * CAP + t
            tile = slot_tile(table, MINE_AT + at, i)
            both = jnp.where(tile >= 0, total[jnp.maximum(tile, 0)] + other[i], 0.0)
            if m >= coded:
                outs[m][t] = both
            else:
                held[t] = both
                most = largest(most, both)
        if m < coded:
            encode(held, most, outs[m])


def code(table, first, last, total, other, plain):
    chunks = last - first
    coded = chunks - plain
    return pl.pallas_call(
        functools.partial(code_kernel, first, coded, plain),
        out_shape=[jax.ShapeDtypeStruct((CAP * BLK + TAIL, BLK), BF16)] * coded
        + [jax.ShapeDtypeStruct((CAP, BLK, BLK), F32)] * plain,
        in_specs=[smem_spec(), vmem_spec(), vmem_spec()],
        out_specs=[vmem_spec()] * chunks,
        scratch_shapes=[pltpu.VMEM((CAP, BLK, BLK), F32)],
        compiler_params=params(CODE_MIB),
        cost_estimate=pl.CostEstimate(
            flops=chunks * CAP * BLK * BLK * 8, bytes_accessed=chunks * CAP * BLK * BLK * 10,
            transcendentals=0),
    )(table, total, other)


def relay_kernel(counts, *refs):
    outs, held = refs[-1 - len(counts):-1], refs[-1]
    at = 0
    for m, count in enumerate(counts):
        before, arrived = refs[at], refs[at + 1:at + 1 + count]
        at += 1 + count
        scales = [scale_of(ref) for ref in arrived]
        most = jnp.zeros((1, BLK), F32)
        for t in range(CAP):
            acc = before[t]
            for ref, scale in zip(arrived, scales):
                acc = acc + decode(ref, t, scale)
            held[t] = acc
            most = largest(most, acc)
        encode(held, most, outs[m])


def relay(groups):
    counts = tuple(len(arrived) for _, arrived in groups)
    args = [v for before, arrived in groups for v in (before, *arrived)]
    return pl.pallas_call(
        functools.partial(relay_kernel, counts),
        out_shape=[jax.ShapeDtypeStruct((CAP * BLK + TAIL, BLK), BF16)] * len(counts),
        in_specs=[vmem_spec()] * len(args),
        out_specs=[vmem_spec()] * len(counts),
        scratch_shapes=[pltpu.VMEM((CAP, BLK, BLK), F32)],
        compiler_params=params(CODE_MIB),
        cost_estimate=pl.CostEstimate(
            flops=len(args) * CAP * BLK * BLK * 8, bytes_accessed=len(args) * CAP * BLK * BLK * 4,
            transcendentals=0),
    )(*args)


def sum_kernel(before, *refs):
    arrived, out = refs[:-1], refs[-1]
    scales = [scale_of(ref) for ref in arrived]
    for t in range(CAP):
        acc = before[t]
        for ref, scale in zip(arrived, scales):
            acc = acc + decode(ref, t, scale)
        out[t] = acc


def add_coded(before, arrived):
    count = len(arrived)
    return pl.pallas_call(
        sum_kernel,
        out_shape=jax.ShapeDtypeStruct((CAP, BLK, BLK), F32),
        in_specs=[vmem_spec()] * (1 + count),
        out_specs=vmem_spec(),
        compiler_params=params(10),
        cost_estimate=pl.CostEstimate(
            flops=count * CAP * BLK * BLK * 8, bytes_accessed=count * CAP * BLK * BLK * 2,
            transcendentals=0),
    )(before, *arrived)


def grad_kernel(ids, last, table, *refs):
    count = len(ids)
    blocks, mine, theirs = refs[:count], refs[count], refs[count + 1]
    before, out, total = refs[count + 2] if last else None, refs[-2], refs[-1]
    side = table[SIDE_AT]
    core = table[SIDE_AT + 1]
    for k, place in enumerate(ids):
        dxh = COLS[place][1]
        first = pl.multiple_of((side if dxh == 0 else 1 - side) * 512, 512)
        for part, half in enumerate((core, 1 - core)):
            rows = pl.multiple_of(table[ROW_AT + half * 16 + place] * 256, 256)
            weights = (mine, theirs)[part][pl.ds(rows, 256), pl.ds(first, 512)]
            made = lax.dot_general(
                blocks[k][...], weights, (((1,), (1,)), ((), ())), preferred_element_type=F32)
            if k > 0:
                made = made + total[part]
            elif last:
                made = made + before[part]
            if k < count - 1:
                total[part] = made
            elif last:
                out[:, pl.ds(pl.multiple_of(half * 256, 256), 256)] = made.astype(out.dtype)
            else:
                out[part] = made


def grad_sum(table, ids, blocks, parts, before=None):
    count = len(ids)
    last = before is not None
    return pl.pallas_call(
        functools.partial(grad_kernel, tuple(ids), last),
        out_shape=jax.ShapeDtypeStruct((512, 512), BF16) if last
        else jax.ShapeDtypeStruct((2, 512, 256), F32),
        in_specs=[smem_spec()] + [vmem_spec()] * (count + 2 + last),
        out_specs=vmem_spec(),
        scratch_shapes=[pltpu.VMEM((2, 512, 256), F32)],
        compiler_params=params(GRAD_MIB),
        cost_estimate=pl.CostEstimate(flops=0, bytes_accessed=0, transcendentals=0),
    )(table, *blocks, *parts, *([before] if last else []))


def join_kernel(*refs):
    first = 0
    for part in refs[:-1]:
        refs[-1][first:first + part.shape[0], :] = part[...]
        first += part.shape[0]


def join(parts):
    rows = sum(part.shape[0] for part in parts)
    return pl.pallas_call(
        join_kernel,
        out_shape=jax.ShapeDtypeStruct((rows, parts[0].shape[1]), parts[0].dtype),
        in_specs=[vmem_spec()] * len(parts),
        out_specs=vmem_spec(),
        compiler_params=params(10),
        cost_estimate=pl.CostEstimate(
            flops=0, bytes_accessed=0, transcendentals=0),
    )(*parts)


def body(inputs, grad_out, weight, blocks, owner):
    row = lax.axis_index("row")
    col = lax.axis_index("col")
    core = lax.axis_index("srv")
    x_lo, y = row // 4, row % 4
    z, x_hi = col // 2, col % 2

    sign = 1 - 2 * core

    def ahead(v):
        return lax.ppermute(v, ("col", "srv"), z_shift(1))

    def back(v):
        return lax.ppermute(v, ("col", "srv"), z_shift(-1))

    def across(v):
        return lax.ppermute(v, "col", X_SWAP)

    def around(v):
        return lax.ppermute(v, ("row", "srv"), y_shift(1))

    def to_row(v, dx, dy):
        return lax.ppermute(v, "row", row_shift(dx, dy))

    def to_core(v):
        return lax.ppermute(v, "srv", CORE_SWAP)

    together = lax.optimization_barrier

    listed = blocks[0]
    owners = owner[0]
    live = listed[:, 0] >= 0
    order = jnp.arange(listed.shape[0], dtype=jnp.int32)
    same = owners[:, None] == owners[None, :]
    earlier = order[None, :] < order[:, None]
    rank = jnp.sum((same & earlier & live[None, :]).astype(jnp.int32), axis=1)
    position = jnp.where(live, owners * CAP + rank, -1)
    tile = jnp.where(live, listed[:, 1] * 4 + listed[:, 0] % 4, 0)
    fills = position[None, :] == order[:, None]
    slots = jnp.sum(jnp.where(fills, tile[None, :] + 1, 0), axis=1) - 1

    z_of = (z + sign * np.array([dz for dz, _ in COLS])) % 8
    col_of = z_of * 2 + (x_hi ^ np.array([dxh for _, dxh in COLS]))
    found = []
    for h in range(2):
        turn = np.array([t for t in range(4) for _ in range(2)])
        ids = (x_lo ^ np.array([dx for _ in range(4) for dx in range(2)])) * 4 + (y - (1 - 2 * h) * turn) % 4
        hit = ids[None, :] == z_of[:, None]
        found.append(jnp.sum(jnp.where(hit, np.arange(8)[None, :], 0), axis=1))
    dest = (x_lo ^ np.array([dx for dx, _ in DESTS])) * 4 + (y + np.array([dy for _, dy in DESTS])) % 4
    table = jnp.concatenate([
        v.astype(jnp.int32)
        for v in (col_of, *found, x_hi[None], core[None], dest * 2 + core, dest * 2 + 1 - core, slots)])
    xt = inputs.T

    half = lax.dynamic_slice_in_dim(weight, core * 256, 256, 0)
    far_half = to_row(half, 1, 0)
    r1, f1, own, table, xt = together((back(grad_out), ahead(grad_out), grad_out, table, xt))

    near_half, far_half, own, now = together((half, far_half, own, table))
    f2, r2 = ahead(f1), back(r1)
    o0 = across(own)
    pair = join([near_half, far_half])
    w1 = around(pair)
    total = dense(None, now, xt, [grad_out, f1, r1], 0)
    r2, f2, total = together((r2, f2, total))

    w1, now = together((w1, table))
    w2 = around(w1)
    total = dense(total, now, xt, [f2, r2, o0], 3)
    f3, r3, of1 = ahead(f2), back(r2), ahead(o0)
    of2, of1, r3, f3, total = together((across(f2), of1, r3, f3, total))

    w2, now = together((w2, table))
    w3 = around(w2)
    total = dense(total, now, xt, [f3, r3, of2], 6)
    or2, or1, f4, total = together((across(r2), back(o0), ahead(f3), total))

    w3, now = together((w3, table))
    mine = join([pair, w1, w2, w3])
    theirs = to_core(mine)
    total = dense(total, now, xt, [f4, of1, or1, or2], 9)
    of3, or3 = ahead(of2), back(or2)
    of4, or3, of3, total = together((across(f4), or3, of3, total))

    total = dense(total, table, xt, [of3, or3, of4], LAST)
    cols = [grad_out, f1, r1, f2, r2, o0, f3, r3, of2, f4, of1, or1, or2, of3, or3, of4]

    theirs, early_table = together((theirs, table))
    parts = [mine, theirs]
    other_early = to_core(pick(early_table, 0, EARLY, total))
    picked_late = pick(early_table, EARLY, 8, total)
    first_half = grad_sum(early_table, range(5), cols[:5], parts)
    first_half, picked_late, early_table = together((first_half, picked_late, early_table))
    early = code(early_table, 0, EARLY, total, other_early, 0)
    *early, picked_late, late_table = together((*early, picked_late, table))
    other_late = to_core(picked_late)
    late = code(late_table, EARLY, 8, total, other_late, 3)
    next_y, last_y, beside, opposite, own = late

    cross = to_row(early[0], 1, 0)
    ups, downs = to_row(early[1], 0, 1), to_row(early[2], 0, 3)
    near = [to_row(next_y, 0, 1), to_row(last_y, 0, 3)]
    beside, opposite = relay([(beside, [ups, downs]), (opposite, [cross])])
    beside, opposite, grad_table = together((beside, opposite, late_table))
    far = [to_row(beside, 1, 0), to_row(opposite, 0, 2)]
    grad_in = grad_sum(grad_table, range(5, 16), cols[5:], parts, first_half)
    own, grad_in = together((own, grad_in))
    pushed = add_coded(own, near)
    pushed = add_coded(pushed, far)
    return grad_in, pushed.reshape(1, CAP, BLK, BLK)


def solution(mesh):
    in_specs = (
        P(("row", "srv"), "col"),
        P(("row", "srv"), "col"),
        P("col", "row"),
        P("col", None, None),
        P("col", None),
    )
    out_specs = (P(("row", "srv"), "col"), P(("row", "srv"), "col", None, None))
    return jax.shard_map(body, mesh=mesh, in_specs=in_specs, out_specs=out_specs, check_vma=False)
```
